32 devices in a mesh: sub: 16 (over z, y, x), grp: 2 (over core).
Axes of the slice: x: 2, y: 2, z: 4, core: 2. Of those that a mesh axis runs over, the one named last changes fastest.
Arguments:
- applied_loads: float32 [128, 3, 64, 128], P(('sub', 'grp')), may hold values from -12 to 12
- labels: int32 [128, 64], P(('sub', 'grp')), may hold values from 0 to 7
- shear_modulus: float32 [8], replicated, may hold values from 0.05 to 0.25
- stiff_ratio: float32 [8], replicated, may hold values from 0.5 to 2
- local_order: int32 [32, 1152], P(('sub', 'grp')), may hold values from 0 to 1151, each once within a row
- local_inverse: bfloat16 [32, 1152, 1152], P(('sub', 'grp')), may hold values from -0.05 to 0.2
- coarse_basis: float32 [32, 4, 1152], P(('sub', 'grp')), may hold values from -0.1875 to 0.1875
- coarse_inverse: float32 [128, 128], P('sub'), may hold values from -0.05 to 0.2
Outputs:
- solution: float32 [128, 3, 64, 128], P(('sub', 'grp'))
- residual: float32 [128, 3, 64, 128], P(('sub', 'grp'))
- coarse_values: float32 [128, 128], P(('sub', 'grp'))
The draws below stay inside these ranges and needn't reach their ends.
Inputs may be any that keep to these rules, and one draw needn't show every extreme that they name: `local_order`: every row holds each number from 0 to 1151 once.
All inputs are finite; a program needn't handle non-finite values.
Results may differ from the reference program's by a relative error of at most 0.0015.
Values sent between devices are 32-bit elements; how exact they have to be, the bound alone decides.
No kernel may reach another device: no remote copies, remote signals or barrier semaphores. Data moves between devices by JAX's collectives and lax.ppermute only.
A program may use at most 64 MiB of HBM per device.

```python
import math
import jax
import jax.numpy as jnp
from jax import lax

NY = 8
NZ = 8
PLANES = 4
RHS = 128
CV_DEV = 4
ITERS = 3
REGIONS = 8
NODES = 64
SUBN = 1152
NPL = 128
NC = 128
DEVICES = 32


def symmetric_draw(key, order, lowest, highest, spread):
    key_diag, key_jitter = jax.random.split(key)
    diagonal = jnp.exp(jax.random.uniform(key_diag, (order,), jnp.float32, math.log(lowest), math.log(highest)))
    jitter = jax.random.normal(key_jitter, (order, order), jnp.float32) * (spread / math.sqrt(order))
    return (jitter + jitter.T) * 0.7071 + jnp.diag(diagonal)


def draw_local_inverse(key, part):
    device_keys = jax.random.split(jax.random.fold_in(key, 11), DEVICES)

    def single(device_key):
        return symmetric_draw(device_key, SUBN, 0.06, 0.12, 0.025).astype(jnp.bfloat16)
    return lax.map(single, device_keys)


def draw_coarse_inverse(key, part):
    return symmetric_draw(jax.random.fold_in(key, 23), NC, 0.08, 0.16, 0.03)


def with_ends(values, key, least, largest):
    place = [jax.random.randint(jax.random.fold_in(key, axis), (), 0, length) for axis, length in enumerate(values.shape)]
    main_axis = values.shape.index(max(values.shape))
    neighbour = place[:main_axis] + [(place[main_axis] + 1) % values.shape[main_axis]] + place[main_axis + 1:]
    return values.at[tuple(place)].set(least).at[tuple(neighbour)].set(largest)


def block_levels(stream_key, extent, shards, low, high):
    factor_of = 1.0
    for axis_at, blocks in shards:
        steps = jax.random.uniform(jax.random.fold_in(jax.random.fold_in(stream_key, 6), axis_at), (blocks,), jnp.float32, low / len(shards), high / len(shards))
        factor_of = factor_of * jnp.repeat(jnp.exp(steps), extent[axis_at] // blocks).reshape((-1,) + (1,) * (len(extent) - 1 - axis_at))
    return factor_of


def bell_draw(rng, dims, scale, bound, cuts=(), kind=jnp.bfloat16):
    loudness = block_levels(rng, dims, cuts, -0.22, 0.18) if cuts else 1.0
    entries = jax.random.normal(rng, dims, jnp.float32) * scale * loudness
    return jnp.minimum(jnp.maximum(entries, -bound), bound).astype(kind)


def setup_inputs(seed: int = 0) -> dict:
    streams_of = jax.random.split(jax.random.key(seed), 9)
    return {
        "applied_loads": bell_draw(streams_of[0], (NPL, 3, NODES, RHS), 2.0, 12.0, ((0, 32),), jnp.float32),
        "labels": with_ends(jax.random.randint(streams_of[1], (NPL, NODES), 0, REGIONS), jax.random.fold_in(streams_of[1], 1), 0, REGIONS - 1).astype(jnp.int32),
        "shear_modulus": jnp.clip(jnp.exp(jax.random.uniform(streams_of[2], (REGIONS,), jnp.float32, math.log(0.05), math.log(0.25))), 0.05, 0.25),
        "stiff_ratio": jnp.clip(jnp.exp(jax.random.uniform(streams_of[3], (REGIONS,), jnp.float32, math.log(0.5), math.log(2.0))), 0.5, 2.0),
        "local_order": jax.vmap(lambda own: jax.random.permutation(own, SUBN))(jax.random.split(streams_of[4], DEVICES)).reshape((DEVICES, SUBN)).astype(jnp.int32),
        "local_inverse": draw_local_inverse(jax.random.fold_in(streams_of[8], 71), 0),
        "coarse_basis": bell_draw(streams_of[6], (DEVICES, CV_DEV, SUBN), SUBN ** -0.5, 0.1875, ((0, 32),), jnp.float32),
        "coarse_inverse": draw_coarse_inverse(jax.random.fold_in(streams_of[8], 71), 0),
    }


RELAXATION = 0.5
PRECISE = lax.Precision.HIGHEST


def shifted(values, shifts):
    window = tuple(slice(1 + offset, values.shape[dimension] - 1 + offset) for dimension, offset in enumerate(shifts))
    return values[window]


def stiffness(displace, shear_ext, normal_ext):
    padded = jnp.pad(displace, ((0, 0), (0, 0), (1, 1), (1, 1), (0, 0)))
    shear_pad = jnp.pad(shear_ext, ((0, 0), (1, 1), (1, 1)))
    normal_pad = jnp.pad(normal_ext, ((0, 0), (1, 1), (1, 1)))
    results = []
    for component in range(3):
        moving = padded[:, component]
        centre = shifted(moving, (0, 0, 0))
        accumulated = jnp.zeros_like(centre)
        for dimension in range(3):
            coefficient = normal_pad if dimension == component else shear_pad
            middle = shifted(coefficient, (0, 0, 0))
            for direction in (-1, 1):
                offsets = tuple(direction if another == dimension else 0 for another in range(3))
                facing = 0.5 * (middle + shifted(coefficient, offsets))
                accumulated = accumulated + facing[..., None] * (centre - shifted(moving, offsets))
        results.append(accumulated)
    return jnp.stack(results, axis=1)


def lookup(labels, shear_modulus, stiff_ratio):
    onehot = (labels[..., None] == jnp.arange(shear_modulus.shape[0], dtype=jnp.int32)).astype(jnp.float32)
    shear_node = jnp.sum(onehot * shear_modulus, axis=-1)
    normal_node = jnp.sum(onehot * (shear_modulus * (2.0 + stiff_ratio)), axis=-1)
    return shear_node, normal_node


def reference(applied_loads, labels, shear_modulus, stiff_ratio, local_order, local_inverse, coarse_basis, coarse_inverse):
    plane_total = applied_loads.shape[0]
    devices = local_inverse.shape[0]
    forces = applied_loads.reshape(plane_total, 3, NY, NZ, RHS)
    shear_node, normal_node = lookup(labels, shear_modulus, stiff_ratio)
    shear_ext = jnp.pad(shear_node.reshape(plane_total, NY, NZ), ((1, 1), (0, 0), (0, 0)))
    normal_ext = jnp.pad(normal_node.reshape(plane_total, NY, NZ), ((1, 1), (0, 0), (0, 0)))
    plane_pad = ((1, 1), (0, 0), (0, 0), (0, 0), (0, 0))

    def operator(displace):
        return stiffness(jnp.pad(displace, plane_pad), shear_ext, normal_ext)

    def solve_single(bundle):
        ordering, inverse, vector, basis_local, values_local = bundle
        local_part = jnp.dot(inverse, vector[ordering], preferred_element_type=jnp.float32)
        spread = jnp.zeros((SUBN, RHS), jnp.float32).at[ordering].set(local_part)
        return spread + jnp.dot(basis_local.T, values_local, precision=PRECISE)

    solution = jnp.zeros_like(forces)
    coarse_values = jnp.zeros((devices * CV_DEV, RHS), jnp.float32)
    for iteration in range(ITERS):
        remaining = forces - operator(solution)
        padded = jnp.pad(remaining, plane_pad)
        middle = padded[1:-1].reshape(devices, PLANES, 3, NY, NZ, RHS)
        left_plane = padded[0:plane_total:PLANES]
        right_plane = padded[PLANES + 1::PLANES]
        windows = jnp.concatenate([left_plane[:, None], middle, right_plane[:, None]], axis=1).reshape(devices, SUBN, RHS)
        coarse_res = jnp.einsum("dkn,dnr->dkr", coarse_basis, windows, precision=PRECISE).reshape(devices * CV_DEV, RHS)
        coarse_values = jnp.dot(coarse_inverse, coarse_res, precision=PRECISE)
        rounded = windows.astype(jnp.bfloat16)
        corrections = lax.map(solve_single, (local_order, local_inverse, rounded, coarse_basis, coarse_values.reshape(devices, CV_DEV, RHS)))
        corrections = corrections.reshape(devices, PLANES + 2, 3, NY, NZ, RHS)
        owned = corrections[:, 1:PLANES + 1]
        owned = owned.at[1:, 0].add(corrections[:-1, PLANES + 1])
        owned = owned.at[:-1, PLANES - 1].add(corrections[1:, 0])
        solution = solution + RELAXATION * owned.reshape(plane_total, 3, NY, NZ, RHS)
    final_residual = forces - operator(solution)
    return (solution.reshape(plane_total, 3, NY * NZ, RHS), final_residual.reshape(plane_total, 3, NY * NZ, RHS), coarse_values)
```

```python
import functools

import jax
import jax.numpy as jnp
from jax import lax
from jax.experimental import pallas as pl
from jax.experimental.pallas import tpu as pltpu
from jax.sharding import PartitionSpec as P

NY = 8
NZ = 8
CV_DEV = 4
ITERS = 3
RELAXATION = 0.5
AXES = ("sub", "grp")
F32 = jnp.float32
BF16 = jnp.bfloat16
VMEM = pl.BlockSpec(memory_space=pltpu.VMEM)
SMEM = pl.BlockSpec(memory_space=pltpu.SMEM)
PARAMS = pltpu.CompilerParams(vmem_limit_bytes=40 * 1024 * 1024)


def lookup(labels, shear_modulus, stiff_ratio):
    onehot = (labels[..., None] == jnp.arange(shear_modulus.shape[0], dtype=jnp.int32)).astype(F32)
    shear_node = jnp.sum(onehot * shear_modulus, axis=-1)
    normal_node = jnp.sum(onehot * (shear_modulus * (2.0 + stiff_ratio)), axis=-1)
    return shear_node, normal_node


def swap_pairs(count):
    near = [(i, i ^ 1) for i in range(count)]
    far = []
    for i in range(1, count - 1, 2):
        far += [(i, i + 1), (i + 1, i)]
    return near, far


def renumber_kernel(order_ref, inverse_ref, out_ref, hot):
    size = inverse_ref.shape[0]
    step = size // 3
    order = order_ref[...]

    def build(i, carry):
        start = pl.multiple_of(i * step, step)
        row = lax.broadcasted_iota(jnp.int32, (step, size), 0) + start
        hot[pl.ds(start, step), :] = jnp.where(row == order, 1.0, 0.0).astype(BF16)
        return carry

    lax.fori_loop(0, 3, build, 0)
    for i in range(3):
        part = slice(i * step, (i + 1) * step)
        columns = lax.dot_general(
            inverse_ref[...], hot[part, :], (((1,), (1,)), ((), ())), preferred_element_type=F32
        ).astype(BF16)
        out_ref[:, part] = jnp.dot(hot[...], columns, preferred_element_type=F32).astype(BF16)


def renumber(order, inverse):
    size = inverse.shape[0]
    return pl.pallas_call(
        renumber_kernel,
        out_shape=jax.ShapeDtypeStruct((size, size), BF16),
        in_specs=[VMEM, VMEM],
        out_specs=VMEM,
        scratch_shapes=[pltpu.VMEM((size, size), BF16)],
        compiler_params=PARAMS,
        cost_estimate=pl.CostEstimate(flops=4 * size**3, bytes_accessed=4 * size * size, transcendentals=0),
    )(order, inverse)


def up_a(u):
    return jnp.concatenate([u[1:], jnp.zeros_like(u[:1])], axis=0)


def down_a(u):
    return jnp.concatenate([jnp.zeros_like(u[:1]), u[:-1]], axis=0)


def up_b(u):
    return pltpu.roll(u, NZ - 1, 1)


def down_b(u):
    return pltpu.roll(u, 1, 1)


def stencil_plane(mats, plane, field):
    b = lax.broadcasted_iota(jnp.int32, (NY, NZ, mats.shape[-1]), 1)
    last, first = b == NZ - 1, b == 0
    near_a, near_b_up, near_b_down, along, diagonal = [], [], [], [], []
    for kind in range(2):
        s = mats[plane, kind]
        half = 0.5 * s
        k_up = 0.5 * up_a(s) + half
        k_down = 0.5 * down_a(s) + half
        b_up = jnp.where(last, 0.0, 0.5 * up_b(s) + half)
        b_down = jnp.where(first, 0.0, 0.5 * down_b(s) + half)
        p_up = 0.5 * mats[plane + 1, kind] + half
        p_down = 0.5 * mats[plane - 1, kind] + half
        near_a.append((k_up, k_down))
        near_b_up.append(b_up)
        near_b_down.append(b_down)
        along.append((p_up, p_down))
        edge = jnp.where(last | first, half, 0.0)
        diagonal.append((p_up + p_down, k_up + k_down, b_up + b_down + edge))
    results = []
    for component in range(3):
        kinds = [1 if dimension == component else 0 for dimension in range(3)]
        u = field(plane, component)
        total = (diagonal[kinds[0]][0] + diagonal[kinds[1]][1] + diagonal[kinds[2]][2]) * u
        total = total - along[kinds[0]][0] * field(plane + 1, component)
        total = total - along[kinds[0]][1] * field(plane - 1, component)
        total = total - near_a[kinds[1]][0] * up_a(u)
        total = total - near_a[kinds[1]][1] * down_a(u)
        total = total - near_b_up[kinds[2]] * up_b(u)
        total = total - near_b_down[kinds[2]] * down_b(u)
        results.append(total)
    return results


def split(x):
    high = x.astype(BF16)
    return high, (x - high.astype(F32)).astype(BF16)


def products(place_ref, inverse_ref, basis_ref, res_ref, t_ref, near_ref, far_ref, q_ref):
    slots, rows, cases = res_ref.shape[0] * 3, NY * NZ, res_ref.shape[-1]
    size = slots * rows
    res = res_ref[...].reshape(size, cases)
    high, low = split(res)
    step = size // 3
    t_planes = t_ref.shape[0]
    for i in range(3):
        block = jnp.dot(inverse_ref[i * step : (i + 1) * step, :], high, preferred_element_type=F32)
        per = t_planes // 3
        t_ref[i * per : (i + 1) * per] = block.reshape(per, 3, NY, NZ, cases)
    even = place_ref[0]
    width = near_ref.shape[0]
    to_right = t_planes - width
    near_ref[...] = t_ref[pl.ds(to_right * even, width)]
    far_ref[...] = t_ref[pl.ds(to_right * (1 - even), width)]
    b_high, b_low = split(basis_ref[...])
    both = jnp.concatenate([b_high, b_low], axis=0)
    first = jnp.dot(both, high, preferred_element_type=F32)
    second = jnp.dot(both, low, preferred_element_type=F32)
    half = basis_ref.shape[0]
    q = (first[:half] + second[:half] + first[half:])[:CV_DEV]
    q_ref[...] = jnp.broadcast_to(q[None], q_ref.shape)


def first_kernel(place_ref, loads_ref, left_ref, right_ref, inverse_ref, basis_ref,
                 res_ref, t_ref, near_ref, far_ref, q_ref):
    planes = loads_ref.shape[0]
    res_ref[0] = left_ref[...]
    res_ref[1 : planes + 1] = loads_ref[...]
    res_ref[planes + 1] = right_ref[...]
    products(place_ref, inverse_ref, basis_ref, res_ref, t_ref, near_ref, far_ref, q_ref)


def correction(place_ref, q_ref, rows_ref, extent_ref, t_ref, near_ref, far_ref, z_ref):
    width = near_ref.shape[0]
    out_planes = t_ref.shape[0] + 2
    cases = t_ref.shape[-1]
    coarse = jnp.dot(rows_ref[...], q_ref[...], precision=lax.Precision.HIGHEST, preferred_element_type=F32)
    c_high, c_low = split(coarse)
    e_high, e_low = split(extent_ref[...])
    spread = lax.dot_general(
        jnp.concatenate([e_high, e_low, e_high], axis=0),
        jnp.concatenate([c_high, c_high, c_low], axis=0),
        (((0,), (0,)), ((), ())),
        preferred_element_type=F32,
    ).reshape(out_planes, 3, NY, NZ, cases)
    even = place_ref[0] == 1
    has_left = place_ref[1].astype(F32)
    has_right = place_ref[2].astype(F32)
    for plane in range(3 - width, out_planes - 3 + width):
        value = spread[plane]
        if 1 <= plane < out_planes - 1:
            value = value + t_ref[plane - 1]
        if plane < 3:
            at = plane - (3 - width)
            value = value + jnp.where(even, far_ref[at], near_ref[at])
        if plane >= out_planes - 3:
            at = plane - (out_planes - 3)
            value = value + jnp.where(even, near_ref[at], far_ref[at])
        if plane < 2:
            value = value * has_left
        if plane >= out_planes - 2:
            value = value * has_right
        z_ref[plane] = value
    return coarse


def middle_kernel(with_solution, place_ref, q_in_ref, rows_ref, extent_ref, mats_ref, t_in_ref, near_in_ref,
                  far_in_ref, res_in_ref, *rest):
    if with_solution:
        solution_in_ref, *rest = rest
    inverse_ref, basis_ref, solution_ref, res_ref, t_ref, near_ref, far_ref, q_ref, z_ref = rest
    correction(place_ref, q_in_ref, rows_ref, extent_ref, t_in_ref, near_in_ref, far_in_ref, z_ref)
    window = res_ref.shape[0]
    for plane in range(1, window + 1):
        applied = stencil_plane(mats_ref, plane, lambda p, c: z_ref[p, c])
        for component in range(3):
            value = res_in_ref[plane - 1, component] - RELAXATION * applied[component]
            if plane == 1:
                value = value * place_ref[1].astype(F32)
            if plane == window:
                value = value * place_ref[2].astype(F32)
            res_ref[plane - 1, component] = value
    own = RELAXATION * z_ref[2 : window]
    solution_ref[...] = solution_in_ref[...] + own if with_solution else own
    products(place_ref, inverse_ref, basis_ref, res_ref, t_ref, near_ref, far_ref, q_ref)


def last_kernel(place_ref, q_in_ref, rows_ref, extent_ref, mats_ref, t_in_ref, near_in_ref, far_in_ref, res_in_ref,
                solution_in_ref, solution_ref, residual_ref, coarse_ref, z_ref):
    coarse = correction(place_ref, q_in_ref, rows_ref, extent_ref, t_in_ref, near_in_ref, far_in_ref, z_ref)
    coarse_ref[...] = coarse[CV_DEV : 2 * CV_DEV]
    planes = solution_ref.shape[0]
    for plane in range(2, planes + 2):
        applied = stencil_plane(mats_ref, plane, lambda p, c: z_ref[p, c])
        for component in range(3):
            residual_ref[plane - 2, component] = (
                res_in_ref[plane - 1, component] - RELAXATION * applied[component]
            )
    solution_ref[...] = solution_in_ref[...] + RELAXATION * z_ref[2 : planes + 2]


def rows_of(matrix):
    k, n = matrix.shape
    blocks = -(-n // 128)
    padded = jnp.pad(matrix, ((0, 0), (0, blocks * 128 - n)))
    return [padded[:, i * 128 : (i + 1) * 128] for i in range(blocks)]


def of_rows(rows, k, n):
    blocks = -(-n // 128)
    return jnp.concatenate([rows[i * k : (i + 1) * k] for i in range(blocks)], axis=1)[:, :n]


def body(
    applied_loads,
    labels,
    shear_modulus,
    stiff_ratio,
    local_order,
    local_inverse,
    coarse_basis,
    coarse_inverse,
):
    planes, components, nodes, cases = applied_loads.shape
    window = planes + 2
    plane_rows = components * nodes
    size = window * plane_rows
    order_coarse = coarse_inverse.shape[1]
    position = lax.axis_index(AXES)
    count = lax.axis_size(AXES)
    even = (position % 2) == 0
    near_pairs, far_pairs = swap_pairs(count)
    place = jnp.stack(
        [even.astype(jnp.int32), (position > 0).astype(jnp.int32), (position < count - 1).astype(jnp.int32)]
    )
    basis = coarse_basis[0]
    own_rows = lax.dynamic_slice_in_dim(coarse_inverse, lax.axis_index("grp") * CV_DEV, CV_DEV, 0)
    mats = jnp.stack(lookup(labels, shear_modulus, stiff_ratio), axis=1)

    part = 3 * plane_rows

    def pack(load_plane, mat_planes, basis_part):
        rows = [load_plane.reshape(plane_rows, cases)]
        rows += rows_of(basis_part) + rows_of(own_rows)
        rows.append(mat_planes.reshape(2 * 2 * nodes // 128, 128))
        return jnp.concatenate(rows, axis=0)

    to_left = pack(applied_loads[0], mats[:2], basis[:, :part])
    to_right = pack(applied_loads[planes - 1], mats[planes - 2 :], basis[:, size - part :])
    near = lax.ppermute(jnp.where(even, to_right, to_left), AXES, near_pairs)
    far = lax.ppermute(jnp.where(even, to_left, to_right), AXES, far_pairs)
    natural = renumber(local_order, local_inverse[0])
    left = jnp.where(even, far, near)
    right = jnp.where(even, near, far)

    def unpack(packed):
        at = plane_rows
        load_plane = packed[:at].reshape(components, NY, NZ, cases)
        basis_rows = CV_DEV * (-(-part // 128))
        basis_part = of_rows(packed[at : at + basis_rows], CV_DEV, part)
        at += basis_rows
        coarse_rows = CV_DEV * (-(-order_coarse // 128))
        inverse_rows = of_rows(packed[at : at + coarse_rows], CV_DEV, order_coarse)
        at += coarse_rows
        return load_plane, basis_part, inverse_rows, packed[at:].reshape(2, 2, nodes)

    left_load, left_basis, left_rows, left_mats = unpack(left)
    right_load, right_basis, right_rows, right_mats = unpack(right)
    mats_all = jnp.concatenate([left_mats, mats, right_mats], axis=0)
    mats_all = jnp.broadcast_to(mats_all[..., None], (planes + 4, 2, nodes, cases))
    mats_all = mats_all.reshape(planes + 4, 2, NY, NZ, cases)
    extent = size + 2 * plane_rows
    extents = jnp.concatenate(
        [
            jnp.pad(left_basis, ((0, 0), (0, extent - part))),
            jnp.pad(basis, ((0, 0), (plane_rows, plane_rows))),
            jnp.pad(right_basis, ((0, CV_DEV), (extent - part, 0))),
        ],
        axis=0,
    )
    inverse_rows = jnp.concatenate([left_rows, own_rows, jnp.pad(right_rows, ((0, CV_DEV), (0, 0)))], axis=0)
    basis_pad = jnp.pad(basis, ((0, 16 - CV_DEV), (0, 0)))

    def field(depth):
        return jax.ShapeDtypeStruct((depth, components, NY, NZ, cases), F32)

    q_shape = jax.ShapeDtypeStruct((count, CV_DEV, cases), F32)
    cost = pl.CostEstimate(flops=2 * size * size * cases, bytes_accessed=2 * size * size, transcendentals=0)
    z_scratch = pltpu.VMEM((planes + 4, components, NY, NZ, cases), F32)
    loads = applied_loads.reshape(planes, components, NY, NZ, cases)

    def move(near_out, far_out, q):
        near_in = lax.ppermute(near_out, AXES, near_pairs)
        far_in = lax.ppermute(far_out, AXES, far_pairs)
        q_all = lax.all_to_all(q, AXES, 0, 0).reshape(count * CV_DEV, cases)
        return near_in, far_in, q_all

    res, t, near_out, far_out, q = pl.pallas_call(
        first_kernel,
        out_shape=[field(window), field(window), field(3), field(3), q_shape],
        in_specs=[SMEM] + [VMEM] * 5,
        out_specs=[VMEM] * 5,
        compiler_params=PARAMS,
        cost_estimate=cost,
    )(place, loads, left_load, right_load, natural, basis_pad)
    near_in, far_in, q_all = move(near_out, far_out, q)
    solution = None
    for iteration in range(1, ITERS):
        width = 2 if iteration == ITERS - 1 else 3
        extra = [] if solution is None else [solution]
        operands = [place, q_all, inverse_rows, extents, mats_all, t, near_in, far_in, res, *extra, natural, basis_pad]
        solution, res, t, near_out, far_out, q = pl.pallas_call(
            functools.partial(middle_kernel, bool(extra)),
            out_shape=[field(planes), field(window), field(window), field(width), field(width), q_shape],
            in_specs=[SMEM] + [VMEM] * (len(operands) - 1),
            out_specs=[VMEM] * 6,
            scratch_shapes=[z_scratch],
            compiler_params=PARAMS,
            cost_estimate=cost,
        )(*operands)
        near_in, far_in, q_all = move(near_out, far_out, q)
    solution, residual, coarse_values = pl.pallas_call(
        last_kernel,
        out_shape=[field(planes), field(planes), jax.ShapeDtypeStruct((CV_DEV, cases), F32)],
        in_specs=[SMEM] + [VMEM] * 9,
        out_specs=[VMEM] * 3,
        scratch_shapes=[z_scratch],
        compiler_params=PARAMS,
    )(place, q_all, inverse_rows, extents, mats_all, t, near_in, far_in, res, solution)
    return (
        solution.reshape(planes, components, nodes, cases),
        residual.reshape(planes, components, nodes, cases),
        coarse_values,
    )


def solution(mesh):
    return jax.shard_map(
        body,
        mesh=mesh,
        in_specs=(
            P(("sub", "grp"), None, None, None),
            P(("sub", "grp"), None),
            P(),
            P(),
            P(("sub", "grp"), None),
            P(("sub", "grp"), None, None),
            P(("sub", "grp"), None, None),
            P("sub", None),
        ),
        out_specs=(
            P(("sub", "grp"), None, None, None),
            P(("sub", "grp"), None, None, None),
            P(("sub", "grp"), None),
        ),
        check_vma=False,
    )
```

```python
import functools

import jax
import jax.numpy as jnp
from jax import lax
from jax.experimental import pallas as pl
from jax.experimental.pallas import tpu as pltpu
from jax.sharding import PartitionSpec as P

NY = 8
NZ = 8
CV_DEV = 4
ITERS = 3
RELAXATION = 0.5
AXES = ("sub", "grp")
F32 = jnp.float32
BF16 = jnp.bfloat16
VMEM = pl.BlockSpec(memory_space=pltpu.VMEM)
SMEM = pl.BlockSpec(memory_space=pltpu.SMEM)
PARAMS = pltpu.CompilerParams(vmem_limit_bytes=24 * 1024 * 1024)


def swap_pairs(count):
    near = [(i, i ^ 1) for i in range(count)]
    far = []
    for i in range(1, count - 1, 2):
        far += [(i, i + 1), (i + 1, i)]
    return near, far


def pack_kernel(place_ref, shear_ref, ratio_ref, loads_ref, labels_ref, wide_ref, coarse_ref,
                near_ref, far_ref, mats_ref, rows_ref):
    planes, nodes = labels_ref.shape
    plane_rows = loads_ref.shape[1] * loads_ref.shape[2]
    even = place_ref[0] == 1
    labels = labels_ref[...]
    shear = jnp.zeros((planes, nodes), F32)
    normal = jnp.zeros((planes, nodes), F32)
    for region in range(shear_ref.shape[0]):
        value = shear_ref[region]
        here = labels == region
        shear = jnp.where(here, value, shear)
        normal = jnp.where(here, value * (2.0 + ratio_ref[region]), normal)
    both = jnp.concatenate([shear, normal], axis=1)
    mats_ref[...] = both
    rows = coarse_ref[:CV_DEV]
    for member in range(1, coarse_ref.shape[0] // CV_DEV):
        rows = jnp.where(place_ref[3] == member, coarse_ref[member * CV_DEV : (member + 1) * CV_DEV], rows)
    rows_ref[...] = rows
    span = part_blocks(plane_rows)
    load_l = loads_ref[0].reshape(plane_rows, loads_ref.shape[3])
    load_r = loads_ref[planes - 1].reshape(plane_rows, loads_ref.shape[3])
    mats_l, mats_r = both[:2], both[planes - 2 :]
    start_r = planes * plane_rows
    start_l = 4 * plane_rows - 128 * span
    near_ref[:plane_rows] = jnp.where(even, load_r, load_l)
    far_ref[:plane_rows] = jnp.where(even, load_l, load_r)
    groups = group_count(plane_rows, coarse_ref.shape[1])
    for i in range(groups):
        at = plane_rows + 8 * i
        if i < span:
            block_l = wide_ref[:, start_l + 128 * i : start_l + 128 * (i + 1)]
            block_r = wide_ref[:, start_r + 128 * i : start_r + 128 * (i + 1)]
            near_ref[at : at + CV_DEV] = jnp.where(even, block_r, block_l)
            far_ref[at : at + CV_DEV] = jnp.where(even, block_l, block_r)
        if i * 128 < coarse_ref.shape[1]:
            near_ref[at + CV_DEV : at + 2 * CV_DEV] = rows[:, 128 * i : 128 * (i + 1)]
            far_ref[at + CV_DEV : at + 2 * CV_DEV] = rows[:, 128 * i : 128 * (i + 1)]
    at = plane_rows + 8 * groups
    near_ref[at : at + 2] = jnp.where(even, mats_r, mats_l)
    far_ref[at : at + 2] = jnp.where(even, mats_l, mats_r)


def part_blocks(plane_rows):
    return -(-3 * plane_rows // 128)


def group_count(plane_rows, coarse_order):
    return max(part_blocks(plane_rows), coarse_order // 128)


def renumber_kernel(order_ref, inverse_ref, out_ref, gather_ref, hot, held, sems):
    size = inverse_ref.shape[0]
    step = size // 3
    copies = []
    for i in range(3):
        part = pl.ds(i * step, step)
        copy = pltpu.make_async_copy(inverse_ref.at[:, part], held.at[:, part], sems.at[i])
        copy.start()
        copies.append(copy)
    order = order_ref[...]
    for i in range(size // 128):
        row = lax.broadcasted_iota(jnp.int32, (128, size), 0) + i * 128
        hot[i * 128 : (i + 1) * 128, :] = jnp.where(row == order, 1.0, 0.0).astype(BF16)
        turned = jnp.transpose(jnp.broadcast_to(order[:, i * 128 : (i + 1) * 128], (128, 128)))
        for k in range(size // 128):
            column = lax.broadcasted_iota(jnp.int32, (128, 128), 1) + k * 128
            gather_ref[i * 128 : (i + 1) * 128, k * 128 : (k + 1) * 128] = jnp.where(
                turned == column, 1.0, 0.0
            ).astype(BF16)
    for i in range(3):
        part = slice(i * step, (i + 1) * step)
        copies[i].wait()
        out_ref[:, part] = jnp.dot(hot[...], held[:, part], preferred_element_type=F32).astype(BF16)


def renumber(order, inverse):
    size = inverse.shape[0]
    square = jax.ShapeDtypeStruct((size, size), BF16)
    return pl.pallas_call(
        renumber_kernel,
        out_shape=[square, square],
        in_specs=[VMEM, pl.BlockSpec(memory_space=pl.ANY)],
        out_specs=[VMEM, VMEM],
        scratch_shapes=[
            pltpu.VMEM((size, size), BF16),
            pltpu.VMEM((size, size), BF16),
            pltpu.SemaphoreType.DMA((3,)),
        ],
        compiler_params=PARAMS,
        cost_estimate=pl.CostEstimate(flops=4 * size**3, bytes_accessed=4 * size * size, transcendentals=0),
    )(order, inverse)


def up_a(u):
    return jnp.concatenate([u[1:], jnp.zeros_like(u[:1])], axis=0)


def down_a(u):
    return jnp.concatenate([jnp.zeros_like(u[:1]), u[:-1]], axis=0)


def up_b(u):
    return pltpu.roll(u, NZ - 1, 1)


def down_b(u):
    return pltpu.roll(u, 1, 1)


def stencil_plane(mats, plane, field):
    b = lax.broadcasted_iota(jnp.int32, (NY, NZ, mats.shape[-1]), 1)
    last, first = b == NZ - 1, b == 0
    near_a, near_b_up, near_b_down, along, diagonal = [], [], [], [], []
    for kind in range(2):
        s = mats[plane, kind]
        half = 0.5 * s
        k_up = 0.5 * up_a(s) + half
        k_down = 0.5 * down_a(s) + half
        b_up = jnp.where(last, 0.0, 0.5 * up_b(s) + half)
        b_down = jnp.where(first, 0.0, 0.5 * down_b(s) + half)
        p_up = 0.5 * mats[plane + 1, kind] + half
        p_down = 0.5 * mats[plane - 1, kind] + half
        near_a.append((k_up, k_down))
        near_b_up.append(b_up)
        near_b_down.append(b_down)
        along.append((p_up, p_down))
        edge = jnp.where(last | first, half, 0.0)
        diagonal.append((p_up + p_down, k_up + k_down, b_up + b_down + edge))
    results = []
    for component in range(3):
        kinds = [1 if dimension == component else 0 for dimension in range(3)]
        u = field(plane, component)
        total = (diagonal[kinds[0]][0] + diagonal[kinds[1]][1] + diagonal[kinds[2]][2]) * u
        total = total - along[kinds[0]][0] * field(plane + 1, component)
        total = total - along[kinds[0]][1] * field(plane - 1, component)
        total = total - near_a[kinds[1]][0] * up_a(u)
        total = total - near_a[kinds[1]][1] * down_a(u)
        total = total - near_b_up[kinds[2]] * up_b(u)
        total = total - near_b_down[kinds[2]] * down_b(u)
        results.append(total)
    return results


def split(x):
    high = x.astype(BF16)
    return high, (x - high.astype(F32)).astype(BF16)


def products(place_ref, inverse_ref, gather_ref, basis_ref, res_ref, t_ref, near_ref, far_ref, q_ref):
    slots, rows, cases = res_ref.shape[0] * 3, NY * NZ, res_ref.shape[-1]
    size = slots * rows
    res = res_ref[...].reshape(size, cases)
    high, low = split(res)
    ordered = jnp.dot(gather_ref[...], high, preferred_element_type=F32).astype(BF16)
    step = size // 3
    t_planes = t_ref.shape[0]
    for i in range(3):
        block = jnp.dot(inverse_ref[i * step : (i + 1) * step, :], ordered, preferred_element_type=F32)
        per = t_planes // 3
        t_ref[i * per : (i + 1) * per] = block.reshape(per, 3, NY, NZ, cases)
    even = place_ref[0]
    width = near_ref.shape[0]
    to_right = t_planes - width
    near_ref[...] = t_ref[pl.ds(to_right * even, width)]
    far_ref[...] = t_ref[pl.ds(to_right * (1 - even), width)]
    b_high, b_low = split(basis_ref[...])
    both = jnp.concatenate([b_high, b_low], axis=0)
    first = jnp.dot(both, high, preferred_element_type=F32)
    second = jnp.dot(both, low, preferred_element_type=F32)
    half = basis_ref.shape[0]
    q = (first[:half] + second[:half] + first[half:])[:CV_DEV]
    q_ref[...] = jnp.broadcast_to(q[None], q_ref.shape)


def first_kernel(place_ref, loads_ref, near_in_ref, far_in_ref, mats_in_ref, wide_ref, own_rows_ref,
                 inverse_ref, gather_ref, basis_ref,
                 res_ref, t_ref, near_ref, far_ref, q_ref, mats_ref, extent_ref, rows_ref):
    planes, components = loads_ref.shape[:2]
    cases = loads_ref.shape[-1]
    plane_rows = components * NY * NZ
    even = place_ref[0] == 1

    def beside(start, stop):
        near, far = near_in_ref[start:stop], far_in_ref[start:stop]
        return jnp.where(even, far, near), jnp.where(even, near, far)

    left, right = beside(0, plane_rows)
    res_ref[0] = left.reshape(components, NY, NZ, cases)
    res_ref[1 : planes + 1] = loads_ref[...]
    res_ref[planes + 1] = right.reshape(components, NY, NZ, cases)
    products(place_ref, inverse_ref, gather_ref, basis_ref, res_ref, t_ref, near_ref, far_ref, q_ref)

    extent = extent_ref.shape[1]
    span = part_blocks(plane_rows)
    extent_ref[...] = jnp.zeros_like(extent_ref)
    rows_ref[...] = jnp.zeros_like(rows_ref)
    extent_ref[CV_DEV : 2 * CV_DEV] = wide_ref[...]
    rows_ref[CV_DEV : 2 * CV_DEV] = own_rows_ref[...]
    groups = group_count(plane_rows, rows_ref.shape[1])
    for i in range(groups):
        at = plane_rows + 8 * i
        if i < span:
            left, right = beside(at, at + CV_DEV)
            extent_ref[:CV_DEV, 128 * i : 128 * (i + 1)] = left
            start = extent - 128 * span + 128 * i
            extent_ref[2 * CV_DEV : 3 * CV_DEV, start : start + 128] = right
        if i * 128 < rows_ref.shape[1]:
            left, right = beside(at + CV_DEV, at + 2 * CV_DEV)
            rows_ref[:CV_DEV, 128 * i : 128 * (i + 1)] = left
            rows_ref[2 * CV_DEV : 3 * CV_DEV, 128 * i : 128 * (i + 1)] = right
    at = plane_rows + 8 * groups
    left, right = beside(at, at + 2)
    everything = [left[0:1], left[1:2]] + [mats_in_ref[p : p + 1] for p in range(planes)] + [right[0:1], right[1:2]]
    for plane, row in enumerate(everything):
        turned = jnp.transpose(jnp.broadcast_to(row, (cases, row.shape[1])))
        mats_ref[plane] = turned.reshape(2, NY, NZ, cases)


def correction(place_ref, q_ref, rows_ref, extent_ref, t_ref, near_ref, far_ref, z_ref):
    width = near_ref.shape[0]
    out_planes = t_ref.shape[0] + 2
    cases = t_ref.shape[-1]
    coarse = jnp.dot(rows_ref[...], q_ref[...], precision=lax.Precision.HIGHEST, preferred_element_type=F32)
    c_high, c_low = split(coarse)
    e_high, e_low = split(extent_ref[...])
    spread = lax.dot_general(
        jnp.concatenate([e_high, e_low, e_high], axis=0),
        jnp.concatenate([c_high, c_high, c_low], axis=0),
        (((0,), (0,)), ((), ())),
        preferred_element_type=F32,
    ).reshape(out_planes, 3, NY, NZ, cases)
    even = place_ref[0] == 1
    has_left = place_ref[1].astype(F32)
    has_right = place_ref[2].astype(F32)
    for plane in range(3 - width, out_planes - 3 + width):
        value = spread[plane]
        if 1 <= plane < out_planes - 1:
            value = value + t_ref[plane - 1]
        if plane < 3:
            at = plane - (3 - width)
            value = value + jnp.where(even, far_ref[at], near_ref[at])
        if plane >= out_planes - 3:
            at = plane - (out_planes - 3)
            value = value + jnp.where(even, near_ref[at], far_ref[at])
        if plane < 2:
            value = value * has_left
        if plane >= out_planes - 2:
            value = value * has_right
        z_ref[plane] = value
    return coarse


def middle_kernel(with_solution, place_ref, q_in_ref, rows_ref, extent_ref, mats_ref, t_in_ref, near_in_ref,
                  far_in_ref, res_in_ref, *rest):
    if with_solution:
        solution_in_ref, *rest = rest
    inverse_ref, gather_ref, basis_ref, solution_ref, res_ref, t_ref, near_ref, far_ref, q_ref, z_ref = rest
    correction(place_ref, q_in_ref, rows_ref, extent_ref, t_in_ref, near_in_ref, far_in_ref, z_ref)
    window = res_ref.shape[0]
    for plane in range(1, window + 1):
        applied = stencil_plane(mats_ref, plane, lambda p, c: z_ref[p, c])
        for component in range(3):
            value = res_in_ref[plane - 1, component] - RELAXATION * applied[component]
            if plane == 1:
                value = value * place_ref[1].astype(F32)
            if plane == window:
                value = value * place_ref[2].astype(F32)
            res_ref[plane - 1, component] = value
    own = RELAXATION * z_ref[2 : window]
    solution_ref[...] = solution_in_ref[...] + own if with_solution else own
    products(place_ref, inverse_ref, gather_ref, basis_ref, res_ref, t_ref, near_ref, far_ref, q_ref)


def last_kernel(place_ref, q_in_ref, rows_ref, extent_ref, mats_ref, t_in_ref, near_in_ref, far_in_ref, res_in_ref,
                solution_in_ref, solution_ref, residual_ref, coarse_ref, z_ref):
    coarse = correction(place_ref, q_in_ref, rows_ref, extent_ref, t_in_ref, near_in_ref, far_in_ref, z_ref)
    coarse_ref[...] = coarse[CV_DEV : 2 * CV_DEV]
    planes = solution_ref.shape[0]
    for plane in range(2, planes + 2):
        applied = stencil_plane(mats_ref, plane, lambda p, c: z_ref[p, c])
        for component in range(3):
            residual_ref[plane - 2, component] = (
                res_in_ref[plane - 1, component] - RELAXATION * applied[component]
            )
    solution_ref[...] = solution_in_ref[...] + RELAXATION * z_ref[2 : planes + 2]


def body(
    applied_loads,
    labels,
    shear_modulus,
    stiff_ratio,
    local_order,
    local_inverse,
    coarse_basis,
    coarse_inverse,
):
    planes, components, nodes, cases = applied_loads.shape
    window = planes + 2
    plane_rows = components * nodes
    size = window * plane_rows
    coarse_order = coarse_inverse.shape[1]
    position = lax.axis_index(AXES)
    count = lax.axis_size(AXES)
    near_pairs, far_pairs = swap_pairs(count)
    place = jnp.stack(
        [
            (position % 2 == 0).astype(jnp.int32),
            (position > 0).astype(jnp.int32),
            (position < count - 1).astype(jnp.int32),
            lax.axis_index("grp").astype(jnp.int32),
        ]
    )
    basis = coarse_basis[0]
    wide = jnp.pad(basis, ((0, 0), (plane_rows, plane_rows)))
    basis_pad = jnp.pad(basis, ((0, 16 - CV_DEV), (0, 0)))
    extent = size + 2 * plane_rows

    packed = jax.ShapeDtypeStruct((plane_rows + 8 * group_count(plane_rows, coarse_order) + 8, cases), F32)
    near_out, far_out, mats_own, own_rows = pl.pallas_call(
        pack_kernel,
        out_shape=[
            packed,
            packed,
            jax.ShapeDtypeStruct((planes, 2 * nodes), F32),
            jax.ShapeDtypeStruct((CV_DEV, coarse_order), F32),
        ],
        in_specs=[SMEM] * 3 + [VMEM] * 4,
        out_specs=[VMEM] * 4,
        compiler_params=PARAMS,
    )(place, shear_modulus, stiff_ratio, applied_loads, labels, wide, coarse_inverse)
    near_in = lax.ppermute(near_out, AXES, near_pairs)
    far_in = lax.ppermute(far_out, AXES, far_pairs)
    ordered_inverse, gather = renumber(local_order, local_inverse[0])

    def field(depth):
        return jax.ShapeDtypeStruct((depth, components, NY, NZ, cases), F32)

    q_shape = jax.ShapeDtypeStruct((count, CV_DEV, cases), F32)
    cost = pl.CostEstimate(flops=2 * size * size * cases, bytes_accessed=2 * size * size, transcendentals=0)
    z_scratch = pltpu.VMEM((planes + 4, components, NY, NZ, cases), F32)
    loads = applied_loads.reshape(planes, components, NY, NZ, cases)

    def move(near_out, far_out, q):
        near_in = lax.ppermute(near_out, AXES, near_pairs)
        far_in = lax.ppermute(far_out, AXES, far_pairs)
        q_all = lax.all_to_all(q, AXES, 0, 0).reshape(count * CV_DEV, cases)
        return near_in, far_in, q_all

    res, t, near_out, far_out, q, mats_all, extents, inverse_rows = pl.pallas_call(
        first_kernel,
        out_shape=[
            field(window),
            field(window),
            field(3),
            field(3),
            q_shape,
            jax.ShapeDtypeStruct((planes + 4, 2, NY, NZ, cases), F32),
            jax.ShapeDtypeStruct((16, extent), F32),
            jax.ShapeDtypeStruct((16, coarse_order), F32),
        ],
        in_specs=[SMEM] + [VMEM] * 9,
        out_specs=[VMEM] * 8,
        compiler_params=PARAMS,
        cost_estimate=cost,
    )(place, loads, near_in, far_in, mats_own, wide, own_rows, ordered_inverse, gather, basis_pad)
    near_in, far_in, q_all = move(near_out, far_out, q)
    solution = None
    for iteration in range(1, ITERS):
        width = 2 if iteration == ITERS - 1 else 3
        extra = [] if solution is None else [solution]
        operands = [place, q_all, inverse_rows, extents, mats_all, t, near_in, far_in, res, *extra,
                    ordered_inverse, gather, basis_pad]
        solution, res, t, near_out, far_out, q = pl.pallas_call(
            functools.partial(middle_kernel, bool(extra)),
            out_shape=[field(planes), field(window), field(window), field(width), field(width), q_shape],
            in_specs=[SMEM] + [VMEM] * (len(operands) - 1),
            out_specs=[VMEM] * 6,
            scratch_shapes=[z_scratch],
            compiler_params=PARAMS,
            cost_estimate=cost,
        )(*operands)
        near_in, far_in, q_all = move(near_out, far_out, q)
    solution, residual, coarse_values = pl.pallas_call(
        last_kernel,
        out_shape=[field(planes), field(planes), jax.ShapeDtypeStruct((CV_DEV, cases), F32)],
        in_specs=[SMEM] + [VMEM] * 9,
        out_specs=[VMEM] * 3,
        scratch_shapes=[z_scratch],
        compiler_params=PARAMS,
    )(place, q_all, inverse_rows, extents, mats_all, t, near_in, far_in, res, solution)
    return (
        solution.reshape(planes, components, nodes, cases),
        residual.reshape(planes, components, nodes, cases),
        coarse_values,
    )


def solution(mesh):
    return jax.shard_map(
        body,
        mesh=mesh,
        in_specs=(
            P(("sub", "grp"), None, None, None),
            P(("sub", "grp"), None),
            P(),
            P(),
            P(("sub", "grp"), None),
            P(("sub", "grp"), None, None),
            P(("sub", "grp"), None, None),
            P("sub", None),
        ),
        out_specs=(
            P(("sub", "grp"), None, None, None),
            P(("sub", "grp"), None, None, None),
            P(("sub", "grp"), None),
        ),
        check_vma=False,
    )
```

```python
import functools

import jax
import jax.numpy as jnp
from jax import lax
from jax.experimental import pallas as pl
from jax.experimental.pallas import tpu as pltpu
from jax.sharding import PartitionSpec as P

NY = 8
NZ = 8
CV_DEV = 4
ITERS = 3
RELAXATION = 0.5
AXES = ("sub", "grp")
F32 = jnp.float32
BF16 = jnp.bfloat16
VMEM = pl.BlockSpec(memory_space=pltpu.VMEM)
HBM = pl.BlockSpec(memory_space=pltpu.HBM)
SMEM = pl.BlockSpec(memory_space=pltpu.SMEM)
PARAMS = pltpu.CompilerParams(vmem_limit_bytes=24 * 1024 * 1024)
WHOLE = pltpu.CompilerParams(vmem_limit_bytes=56 * 1024 * 1024)
MOST = pltpu.CompilerParams(vmem_limit_bytes=50 * 1024 * 1024)


def swap_pairs(count):
    near = [(i, i ^ 1) for i in range(count)]
    far = []
    for i in range(1, count - 1, 2):
        far += [(i, i + 1), (i + 1, i)]
    return near, far


def pack_kernel(place_ref, shear_hbm, ratio_hbm, loads_hbm, labels_hbm, basis_hbm, coarse_hbm,
                near_ref, far_ref, mats_ref, rows_ref, wide_ref,
                shear_ref, ratio_ref, near_load, far_load, labels_ref, basis_ref, coarse_ref, sems):
    planes, nodes = labels_ref.shape
    plane_rows, cases = near_load.shape[0] * near_load.shape[1], near_load.shape[2]
    even = place_ref[0]
    moves = [
        (labels_hbm, labels_ref),
        (shear_hbm, shear_ref),
        (ratio_hbm, ratio_ref),
        (basis_hbm, basis_ref),
        (coarse_hbm, coarse_ref),
        (loads_hbm.at[(planes - 1) * even], near_load),
        (loads_hbm.at[(planes - 1) * (1 - even)], far_load),
    ]
    copies = [pltpu.make_async_copy(source, target, sems.at[i]) for i, (source, target) in enumerate(moves)]
    for copy in copies:
        copy.start()
    even = even == 1
    wide_ref[...] = jnp.zeros_like(wide_ref)
    for copy in copies[:3]:
        copy.wait()
    labels = labels_ref[...]
    shear = jnp.zeros((planes, nodes), F32)
    normal = jnp.zeros((planes, nodes), F32)
    for region in range(shear_ref.shape[1]):
        value = shear_ref[:, region : region + 1]
        here = labels == region
        shear = jnp.where(here, value, shear)
        normal = jnp.where(here, value * (2.0 + ratio_ref[:, region : region + 1]), normal)
    both = jnp.concatenate([shear, normal], axis=1)
    mats_ref[...] = both
    mats_l, mats_r = both[:2], both[planes - 2 :]
    groups = group_count(plane_rows, coarse_ref.shape[1])
    at = plane_rows + 8 * groups
    near_ref[at : at + 2] = jnp.where(even, mats_r, mats_l)
    far_ref[at : at + 2] = jnp.where(even, mats_l, mats_r)
    for copy in copies[3:5]:
        copy.wait()
    wide_ref[:, plane_rows : plane_rows + basis_ref.shape[1]] = basis_ref[...]
    rows = coarse_ref[:CV_DEV]
    for member in range(1, coarse_ref.shape[0] // CV_DEV):
        rows = jnp.where(place_ref[3] == member, coarse_ref[member * CV_DEV : (member + 1) * CV_DEV], rows)
    rows_ref[...] = rows
    span = part_blocks(plane_rows)
    start_r = planes * plane_rows
    start_l = 4 * plane_rows - 128 * span
    for i in range(groups):
        at = plane_rows + 8 * i
        if i < span:
            block_l = wide_ref[:, start_l + 128 * i : start_l + 128 * (i + 1)]
            block_r = wide_ref[:, start_r + 128 * i : start_r + 128 * (i + 1)]
            near_ref[at : at + CV_DEV] = jnp.where(even, block_r, block_l)
            far_ref[at : at + CV_DEV] = jnp.where(even, block_l, block_r)
        if i * 128 < coarse_ref.shape[1]:
            near_ref[at + CV_DEV : at + 2 * CV_DEV] = rows[:, 128 * i : 128 * (i + 1)]
            far_ref[at + CV_DEV : at + 2 * CV_DEV] = rows[:, 128 * i : 128 * (i + 1)]
    for copy in copies[5:]:
        copy.wait()
    near_ref[:plane_rows] = near_load[...].reshape(plane_rows, cases)
    far_ref[:plane_rows] = far_load[...].reshape(plane_rows, cases)


def part_blocks(plane_rows):
    return -(-3 * plane_rows // 128)


def group_count(plane_rows, coarse_order):
    return max(part_blocks(plane_rows), coarse_order // 128)


def renumber_kernel(order_ref, inverse_hbm, out_ref, hot, held, columns, sems):
    size = held.shape[0]
    step = size // 3
    copies = []
    for i in range(3):
        part = pl.ds(i * step, step)
        copy = pltpu.make_async_copy(inverse_hbm.at[part, :], held.at[part, :], sems.at[i])
        copy.start()
        copies.append(copy)
    order = order_ref[...]
    for i in range(size // 128):
        row = lax.broadcasted_iota(jnp.int32, (128, size), 0) + i * 128
        hot[i * 128 : (i + 1) * 128, :] = jnp.where(row == order, 1.0, 0.0).astype(BF16)
    for i in range(3):
        part = slice(i * step, (i + 1) * step)
        copies[i].wait()
        columns[part, :] = lax.dot_general(
            held[part, :], hot[...], (((1,), (1,)), ((), ())), preferred_element_type=F32
        ).astype(BF16)
    for i in range(3):
        part = slice(i * step, (i + 1) * step)
        out_ref[part, :] = jnp.dot(hot[part, :], columns[...], preferred_element_type=F32).astype(BF16)


def renumber(order, inverse):
    size = inverse.shape[0]
    square = pltpu.VMEM((size, size), BF16)
    return pl.pallas_call(
        renumber_kernel,
        out_shape=jax.ShapeDtypeStruct((size, size), BF16),
        in_specs=[VMEM, HBM],
        out_specs=VMEM,
        scratch_shapes=[square, square, square, pltpu.SemaphoreType.DMA((3,))],
        compiler_params=MOST,
        cost_estimate=pl.CostEstimate(flops=4 * size**3, bytes_accessed=4 * size * size, transcendentals=0),
    )(order, inverse)


def up_a(u):
    return jnp.concatenate([u[1:], jnp.zeros_like(u[:1])], axis=0)


def down_a(u):
    return jnp.concatenate([jnp.zeros_like(u[:1]), u[:-1]], axis=0)


def up_b(u):
    return pltpu.roll(u, NZ - 1, 1)


def down_b(u):
    return pltpu.roll(u, 1, 1)


def stencil_plane(mats, plane, field):
    b = lax.broadcasted_iota(jnp.int32, (NY, NZ, mats.shape[-1]), 1)
    last, first = b == NZ - 1, b == 0
    near_a, near_b_up, near_b_down, along, diagonal = [], [], [], [], []
    for kind in range(2):
        s = mats[plane, kind]
        half = 0.5 * s
        k_up = 0.5 * up_a(s) + half
        k_down = 0.5 * down_a(s) + half
        b_up = jnp.where(last, 0.0, 0.5 * up_b(s) + half)
        b_down = jnp.where(first, 0.0, 0.5 * down_b(s) + half)
        p_up = 0.5 * mats[plane + 1, kind] + half
        p_down = 0.5 * mats[plane - 1, kind] + half
        near_a.append((k_up, k_down))
        near_b_up.append(b_up)
        near_b_down.append(b_down)
        along.append((p_up, p_down))
        edge = jnp.where(last | first, half, 0.0)
        diagonal.append((p_up + p_down, k_up + k_down, b_up + b_down + edge))
    results = []
    for component in range(3):
        kinds = [1 if dimension == component else 0 for dimension in range(3)]
        u = field(plane, component)
        total = (diagonal[kinds[0]][0] + diagonal[kinds[1]][1] + diagonal[kinds[2]][2]) * u
        total = total - along[kinds[0]][0] * field(plane + 1, component)
        total = total - along[kinds[0]][1] * field(plane - 1, component)
        total = total - near_a[kinds[1]][0] * up_a(u)
        total = total - near_a[kinds[1]][1] * down_a(u)
        total = total - near_b_up[kinds[2]] * up_b(u)
        total = total - near_b_down[kinds[2]] * down_b(u)
        results.append(total)
    return results


def split(x):
    high = x.astype(BF16)
    return high, (x - high.astype(F32)).astype(BF16)


def products(place_ref, inverse_ref, basis_ref, res_ref, t_ref, near_ref, far_ref, q_ref):
    slots, rows, cases = res_ref.shape[0] * 3, NY * NZ, res_ref.shape[-1]
    size = slots * rows
    res = res_ref[...].reshape(size, cases)
    high, low = split(res)
    step = size // 3
    t_planes = t_ref.shape[0]
    for i in range(3):
        block = jnp.dot(inverse_ref[i * step : (i + 1) * step, :], high, preferred_element_type=F32)
        per = t_planes // 3
        t_ref[i * per : (i + 1) * per] = block.reshape(per, 3, NY, NZ, cases)
    even = place_ref[0]
    width = near_ref.shape[0]
    to_right = t_planes - width
    near_ref[...] = t_ref[pl.ds(to_right * even, width)]
    far_ref[...] = t_ref[pl.ds(to_right * (1 - even), width)]
    b_high, b_low = split(basis_ref[...])
    both = jnp.concatenate([b_high, b_low], axis=0)
    first = jnp.dot(both, high, preferred_element_type=F32)
    second = jnp.dot(both, low, preferred_element_type=F32)
    half = basis_ref.shape[0]
    q = (first[:half] + second[:half] + first[half:])[:CV_DEV]
    q_ref[...] = jnp.broadcast_to(q[None], q_ref.shape)


def first_kernel(place_ref, loads_ref, near_in_ref, far_in_ref, mats_in_ref, wide_ref, own_rows_ref,
                 inverse_ref, basis_ref,
                 res_ref, t_ref, near_ref, far_ref, q_ref, mats_ref, extent_ref, rows_ref):
    planes, components = loads_ref.shape[:2]
    cases = loads_ref.shape[-1]
    plane_rows = components * NY * NZ
    even = place_ref[0] == 1

    def beside(start, stop):
        near, far = near_in_ref[start:stop], far_in_ref[start:stop]
        return jnp.where(even, far, near), jnp.where(even, near, far)

    left, right = beside(0, plane_rows)
    res_ref[0] = left.reshape(components, NY, NZ, cases)
    res_ref[1 : planes + 1] = loads_ref[...]
    res_ref[planes + 1] = right.reshape(components, NY, NZ, cases)
    products(place_ref, inverse_ref, basis_ref, res_ref, t_ref, near_ref, far_ref, q_ref)

    extent = extent_ref.shape[1]
    span = part_blocks(plane_rows)
    extent_ref[...] = jnp.zeros_like(extent_ref)
    rows_ref[...] = jnp.zeros_like(rows_ref)
    extent_ref[CV_DEV : 2 * CV_DEV] = wide_ref[...]
    rows_ref[CV_DEV : 2 * CV_DEV] = own_rows_ref[...]
    groups = group_count(plane_rows, rows_ref.shape[1])
    for i in range(groups):
        at = plane_rows + 8 * i
        if i < span:
            left, right = beside(at, at + CV_DEV)
            extent_ref[:CV_DEV, 128 * i : 128 * (i + 1)] = left
            start = extent - 128 * span + 128 * i
            extent_ref[2 * CV_DEV : 3 * CV_DEV, start : start + 128] = right
        if i * 128 < rows_ref.shape[1]:
            left, right = beside(at + CV_DEV, at + 2 * CV_DEV)
            rows_ref[:CV_DEV, 128 * i : 128 * (i + 1)] = left
            rows_ref[2 * CV_DEV : 3 * CV_DEV, 128 * i : 128 * (i + 1)] = right
    at = plane_rows + 8 * groups
    left, right = beside(at, at + 2)
    everything = [left[0:1], left[1:2]] + [mats_in_ref[p : p + 1] for p in range(planes)] + [right[0:1], right[1:2]]
    for plane, row in enumerate(everything):
        turned = jnp.transpose(jnp.broadcast_to(row, (cases, row.shape[1])))
        mats_ref[plane] = turned.reshape(2, NY, NZ, cases)


def correction(place_ref, q_ref, rows_ref, extent_ref, t_ref, near_ref, far_ref, z_ref):
    width = near_ref.shape[0]
    out_planes = t_ref.shape[0] + 2
    cases = t_ref.shape[-1]
    coarse = jnp.dot(rows_ref[...], q_ref[...], precision=lax.Precision.HIGHEST, preferred_element_type=F32)
    c_high, c_low = split(coarse)
    e_high, e_low = split(extent_ref[...])
    spread = lax.dot_general(
        jnp.concatenate([e_high, e_low, e_high], axis=0),
        jnp.concatenate([c_high, c_high, c_low], axis=0),
        (((0,), (0,)), ((), ())),
        preferred_element_type=F32,
    ).reshape(out_planes, 3, NY, NZ, cases)
    even = place_ref[0] == 1
    has_left = place_ref[1].astype(F32)
    has_right = place_ref[2].astype(F32)
    for plane in range(3 - width, out_planes - 3 + width):
        value = spread[plane]
        if 1 <= plane < out_planes - 1:
            value = value + t_ref[plane - 1]
        if plane < 3:
            at = plane - (3 - width)
            value = value + jnp.where(even, far_ref[at], near_ref[at])
        if plane >= out_planes - 3:
            at = plane - (out_planes - 3)
            value = value + jnp.where(even, near_ref[at], far_ref[at])
        if plane < 2:
            value = value * has_left
        if plane >= out_planes - 2:
            value = value * has_right
        z_ref[plane] = value
    return coarse


def middle_kernel(with_solution, place_ref, q_in_ref, rows_ref, extent_ref, mats_ref, t_in_ref, near_in_ref,
                  far_in_ref, res_in_ref, *rest):
    if with_solution:
        solution_in_ref, *rest = rest
    inverse_ref, basis_ref, solution_ref, res_ref, t_ref, near_ref, far_ref, q_ref, z_ref = rest
    correction(place_ref, q_in_ref, rows_ref, extent_ref, t_in_ref, near_in_ref, far_in_ref, z_ref)
    window = res_ref.shape[0]
    for plane in range(1, window + 1):
        applied = stencil_plane(mats_ref, plane, lambda p, c: z_ref[p, c])
        for component in range(3):
            value = res_in_ref[plane - 1, component] - RELAXATION * applied[component]
            if plane == 1:
                value = value * place_ref[1].astype(F32)
            if plane == window:
                value = value * place_ref[2].astype(F32)
            res_ref[plane - 1, component] = value
    own = RELAXATION * z_ref[2 : window]
    solution_ref[...] = solution_in_ref[...] + own if with_solution else own
    products(place_ref, inverse_ref, basis_ref, res_ref, t_ref, near_ref, far_ref, q_ref)


def last_kernel(place_ref, q_in_ref, rows_ref, extent_ref, mats_ref, t_in_ref, near_in_ref, far_in_ref, res_in_ref,
                solution_in_ref, solution_ref, residual_ref, coarse_ref, z_ref):
    coarse = correction(place_ref, q_in_ref, rows_ref, extent_ref, t_in_ref, near_in_ref, far_in_ref, z_ref)
    coarse_ref[...] = coarse[CV_DEV : 2 * CV_DEV]
    planes = solution_ref.shape[0]
    for plane in range(2, planes + 2):
        applied = stencil_plane(mats_ref, plane, lambda p, c: z_ref[p, c])
        for component in range(3):
            residual_ref[plane - 2, component] = (
                res_in_ref[plane - 1, component] - RELAXATION * applied[component]
            )
    solution_ref[...] = solution_in_ref[...] + RELAXATION * z_ref[2 : planes + 2]


def body(
    applied_loads,
    labels,
    shear_modulus,
    stiff_ratio,
    local_order,
    local_inverse,
    coarse_basis,
    coarse_inverse,
):
    planes, components, nodes, cases = applied_loads.shape
    window = planes + 2
    plane_rows = components * nodes
    size = window * plane_rows
    coarse_order = coarse_inverse.shape[1]
    position = lax.axis_index(AXES)
    count = lax.axis_size(AXES)
    near_pairs, far_pairs = swap_pairs(count)
    place = jnp.stack(
        [
            (position % 2 == 0).astype(jnp.int32),
            (position > 0).astype(jnp.int32),
            (position < count - 1).astype(jnp.int32),
            lax.axis_index("grp").astype(jnp.int32),
        ]
    )
    basis = coarse_basis[0]
    basis_pad = jnp.pad(basis, ((0, 16 - CV_DEV), (0, 0)))
    extent = size + 2 * plane_rows

    packed = jax.ShapeDtypeStruct((plane_rows + 8 * group_count(plane_rows, coarse_order) + 8, cases), F32)
    near_out, far_out, mats_own, own_rows, wide = pl.pallas_call(
        pack_kernel,
        out_shape=[
            packed,
            packed,
            jax.ShapeDtypeStruct((planes, 2 * nodes), F32),
            jax.ShapeDtypeStruct((CV_DEV, coarse_order), F32),
            jax.ShapeDtypeStruct((CV_DEV, extent), F32),
        ],
        in_specs=[SMEM] + [HBM] * 6,
        out_specs=[VMEM] * 5,
        scratch_shapes=[
            pltpu.VMEM((1, shear_modulus.shape[0]), F32),
            pltpu.VMEM((1, shear_modulus.shape[0]), F32),
            pltpu.VMEM((components, nodes, cases), F32),
            pltpu.VMEM((components, nodes, cases), F32),
            pltpu.VMEM((planes, nodes), jnp.int32),
            pltpu.VMEM((CV_DEV, size), F32),
            pltpu.VMEM(coarse_inverse.shape, F32),
            pltpu.SemaphoreType.DMA((7,)),
        ],
        compiler_params=WHOLE,
    )(place, shear_modulus[None], stiff_ratio[None], applied_loads, labels, basis, coarse_inverse)
    near_in = lax.ppermute(near_out, AXES, near_pairs)
    far_in = lax.ppermute(far_out, AXES, far_pairs)
    natural = renumber(local_order, local_inverse[0])

    def field(depth):
        return jax.ShapeDtypeStruct((depth, components, NY, NZ, cases), F32)

    q_shape = jax.ShapeDtypeStruct((count, CV_DEV, cases), F32)
    cost = pl.CostEstimate(flops=2 * size * size * cases, bytes_accessed=2 * size * size, transcendentals=0)
    z_scratch = pltpu.VMEM((planes + 4, components, NY, NZ, cases), F32)
    loads = applied_loads.reshape(planes, components, NY, NZ, cases)

    def move(near_out, far_out, q):
        near_in = lax.ppermute(near_out, AXES, near_pairs)
        far_in = lax.ppermute(far_out, AXES, far_pairs)
        q_all = lax.all_to_all(q, AXES, 0, 0).reshape(count * CV_DEV, cases)
        return near_in, far_in, q_all

    res, t, near_out, far_out, q, mats_all, extents, inverse_rows = pl.pallas_call(
        first_kernel,
        out_shape=[
            field(window),
            field(window),
            field(3),
            field(3),
            q_shape,
            jax.ShapeDtypeStruct((planes + 4, 2, NY, NZ, cases), F32),
            jax.ShapeDtypeStruct((16, extent), F32),
            jax.ShapeDtypeStruct((16, coarse_order), F32),
        ],
        in_specs=[SMEM] + [VMEM] * 8,
        out_specs=[VMEM] * 8,
        compiler_params=PARAMS,
        cost_estimate=cost,
    )(place, loads, near_in, far_in, mats_own, wide, own_rows, natural, basis_pad)
    near_in, far_in, q_all = move(near_out, far_out, q)
    solution = None
    for iteration in range(1, ITERS):
        width = 2 if iteration == ITERS - 1 else 3
        extra = [] if solution is None else [solution]
        operands = [place, q_all, inverse_rows, extents, mats_all, t, near_in, far_in, res, *extra,
                    natural, basis_pad]
        solution, res, t, near_out, far_out, q = pl.pallas_call(
            functools.partial(middle_kernel, bool(extra)),
            out_shape=[field(planes), field(window), field(window), field(width), field(width), q_shape],
            in_specs=[SMEM] + [VMEM] * (len(operands) - 1),
            out_specs=[VMEM] * 6,
            scratch_shapes=[z_scratch],
            compiler_params=PARAMS,
            cost_estimate=cost,
        )(*operands)
        near_in, far_in, q_all = move(near_out, far_out, q)
    solution, residual, coarse_values = pl.pallas_call(
        last_kernel,
        out_shape=[field(planes), field(planes), jax.ShapeDtypeStruct((CV_DEV, cases), F32)],
        in_specs=[SMEM] + [VMEM] * 9,
        out_specs=[VMEM] * 3,
        scratch_shapes=[z_scratch],
        compiler_params=PARAMS,
    )(place, q_all, inverse_rows, extents, mats_all, t, near_in, far_in, res, solution)
    return (
        solution.reshape(planes, components, nodes, cases),
        residual.reshape(planes, components, nodes, cases),
        coarse_values,
    )


def solution(mesh):
    return jax.shard_map(
        body,
        mesh=mesh,
        in_specs=(
            P(("sub", "grp"), None, None, None),
            P(("sub", "grp"), None),
            P(),
            P(),
            P(("sub", "grp"), None),
            P(("sub", "grp"), None, None),
            P(("sub", "grp"), None, None),
            P("sub", None),
        ),
        out_specs=(
            P(("sub", "grp"), None, None, None),
            P(("sub", "grp"), None, None, None),
            P(("sub", "grp"), None),
        ),
        check_vma=False,
    )
```

```python
import functools

import jax
import jax.numpy as jnp
from jax import lax
from jax.experimental import pallas as pl
from jax.experimental.pallas import tpu as pltpu
from jax.sharding import PartitionSpec as P

NY = 8
NZ = 8
CV_DEV = 4
ITERS = 3
RELAXATION = 0.5
AXES = ("sub", "grp")
F32 = jnp.float32
BF16 = jnp.bfloat16
VMEM = pl.BlockSpec(memory_space=pltpu.VMEM)
HBM = pl.BlockSpec(memory_space=pltpu.HBM)
SMEM = pl.BlockSpec(memory_space=pltpu.SMEM)
PARAMS = pltpu.CompilerParams(vmem_limit_bytes=24 * 1024 * 1024)
STAGE = pltpu.CompilerParams(vmem_limit_bytes=50 * 1024 * 1024)
WHOLE = pltpu.CompilerParams(vmem_limit_bytes=56 * 1024 * 1024)


def position():
    place = lax.axis_index(AXES)
    even = 1 - lax.rem(place, 2)
    has_left = (place > 0).astype(F32)
    has_right = (place < lax.axis_size(AXES) - 1).astype(F32)
    return even, has_left, has_right


def swap_pairs(count):
    near = [(i, i ^ 1) for i in range(count)]
    far = []
    for i in range(1, count - 1, 2):
        far += [(i, i + 1), (i + 1, i)]
    return near, far


def pack_kernel(shear_hbm, ratio_hbm, loads_hbm, labels_hbm, basis_hbm, coarse_hbm,
                near_ref, far_ref, mats_ref, rows_ref, wide_ref,
                shear_ref, ratio_ref, near_load, far_load, labels_ref, basis_ref, coarse_ref, sems):
    planes, nodes = labels_ref.shape
    plane_rows, cases = near_load.shape[0] * near_load.shape[1], near_load.shape[2]
    even, _, _ = position()
    moves = [
        (labels_hbm, labels_ref),
        (shear_hbm, shear_ref),
        (ratio_hbm, ratio_ref),
        (basis_hbm, basis_ref),
        (coarse_hbm, coarse_ref),
        (loads_hbm.at[(planes - 1) * even], near_load),
        (loads_hbm.at[(planes - 1) * (1 - even)], far_load),
    ]
    copies = [pltpu.make_async_copy(source, target, sems.at[i]) for i, (source, target) in enumerate(moves)]
    for copy in copies:
        copy.start()
    even = even == 1
    wide_ref[...] = jnp.zeros_like(wide_ref)
    for copy in copies[:3]:
        copy.wait()
    labels = labels_ref[...]
    shear = jnp.zeros((planes, nodes), F32)
    normal = jnp.zeros((planes, nodes), F32)
    for region in range(shear_ref.shape[1]):
        value = shear_ref[:, region : region + 1]
        here = labels == region
        shear = jnp.where(here, value, shear)
        normal = jnp.where(here, value * (2.0 + ratio_ref[:, region : region + 1]), normal)
    both = jnp.concatenate([shear, normal], axis=1)
    mats_ref[...] = both
    mats_l, mats_r = both[:2], both[planes - 2 :]
    groups = group_count(plane_rows, coarse_ref.shape[1])
    at = plane_rows + 8 * groups
    near_ref[at : at + 2] = jnp.where(even, mats_r, mats_l)
    far_ref[at : at + 2] = jnp.where(even, mats_l, mats_r)
    for copy in copies[3:5]:
        copy.wait()
    wide_ref[:, plane_rows : plane_rows + basis_ref.shape[1]] = basis_ref[...]
    rows = coarse_ref[:CV_DEV]
    for member in range(1, coarse_ref.shape[0] // CV_DEV):
        rows = jnp.where(lax.axis_index("grp") == member, coarse_ref[member * CV_DEV : (member + 1) * CV_DEV], rows)
    rows_ref[...] = rows
    span = part_blocks(plane_rows)
    start_r = planes * plane_rows
    start_l = 4 * plane_rows - 128 * span
    for i in range(groups):
        at = plane_rows + 8 * i
        if i < span:
            block_l = wide_ref[:, start_l + 128 * i : start_l + 128 * (i + 1)]
            block_r = wide_ref[:, start_r + 128 * i : start_r + 128 * (i + 1)]
            near_ref[at : at + CV_DEV] = jnp.where(even, block_r, block_l)
            far_ref[at : at + CV_DEV] = jnp.where(even, block_l, block_r)
        if i * 128 < coarse_ref.shape[1]:
            near_ref[at + CV_DEV : at + 2 * CV_DEV] = rows[:, 128 * i : 128 * (i + 1)]
            far_ref[at + CV_DEV : at + 2 * CV_DEV] = rows[:, 128 * i : 128 * (i + 1)]
    for copy in copies[5:]:
        copy.wait()
    near_ref[:plane_rows] = near_load[...].reshape(plane_rows, cases)
    far_ref[:plane_rows] = far_load[...].reshape(plane_rows, cases)


def stage_kernel(inverse_hbm, inverse_ref, sems):
    step = inverse_ref.shape[0] // 3
    copies = []
    for i in range(3):
        part = pl.ds(i * step, step)
        copies.append(pltpu.make_async_copy(inverse_hbm.at[part, :], inverse_ref.at[part, :], sems.at[i]))
    for copy in copies:
        copy.start()
    for copy in copies:
        copy.wait()


def on_lanes(row, shape):
    return jnp.transpose(jnp.broadcast_to(row, (shape[-1], row.shape[1]))).reshape(shape[1:])


def part_blocks(plane_rows):
    return -(-3 * plane_rows // 128)


def group_count(plane_rows, coarse_order):
    return max(part_blocks(plane_rows), coarse_order // 128)


def up_a(u):
    return jnp.concatenate([u[1:], jnp.zeros_like(u[:1])], axis=0)


def down_a(u):
    return jnp.concatenate([jnp.zeros_like(u[:1]), u[:-1]], axis=0)


def up_b(u):
    return pltpu.roll(u, NZ - 1, 1)


def down_b(u):
    return pltpu.roll(u, 1, 1)


def stencil_plane(mats, plane, field):
    b = lax.broadcasted_iota(jnp.int32, (NY, NZ, mats.shape[-1]), 1)
    last, first = b == NZ - 1, b == 0
    near_a, near_b_up, near_b_down, along, diagonal = [], [], [], [], []
    for kind in range(2):
        s = mats[plane, kind]
        half = 0.5 * s
        k_up = 0.5 * up_a(s) + half
        k_down = 0.5 * down_a(s) + half
        b_up = jnp.where(last, 0.0, 0.5 * up_b(s) + half)
        b_down = jnp.where(first, 0.0, 0.5 * down_b(s) + half)
        p_up = 0.5 * mats[plane + 1, kind] + half
        p_down = 0.5 * mats[plane - 1, kind] + half
        near_a.append((k_up, k_down))
        near_b_up.append(b_up)
        near_b_down.append(b_down)
        along.append((p_up, p_down))
        edge = jnp.where(last | first, half, 0.0)
        diagonal.append((p_up + p_down, k_up + k_down, b_up + b_down + edge))
    results = []
    for component in range(3):
        kinds = [1 if dimension == component else 0 for dimension in range(3)]
        u = field(plane, component)
        total = (diagonal[kinds[0]][0] + diagonal[kinds[1]][1] + diagonal[kinds[2]][2]) * u
        total = total - along[kinds[0]][0] * field(plane + 1, component)
        total = total - along[kinds[0]][1] * field(plane - 1, component)
        total = total - near_a[kinds[1]][0] * up_a(u)
        total = total - near_a[kinds[1]][1] * down_a(u)
        total = total - near_b_up[kinds[2]] * up_b(u)
        total = total - near_b_down[kinds[2]] * down_b(u)
        results.append(total)
    return results


def split(x):
    high = x.astype(BF16)
    return high, (x - high.astype(F32)).astype(BF16)


def block(plane, component):
    start = (plane * 3 + component) * NY * NZ
    return slice(start, start + NY * NZ)


def node_grid(rows):
    return rows.reshape(rows.shape[0] // (NY * NZ), NY, NZ, rows.shape[1])


def products(order_ref, inverse_ref, basis_ref, ordered_ref, product_ref, res_ref, t_ref, near_ref, far_ref, q_ref):
    size = res_ref.shape[0]
    for row in range(size):
        ordered_ref[row : row + 1, :] = res_ref[pl.ds(order_ref[0, row], 1), :]
    ordered = ordered_ref[...].astype(BF16)
    step = size // 3
    for i in range(3):
        part = slice(i * step, (i + 1) * step)
        product_ref[part, :] = jnp.dot(inverse_ref[part, :], ordered, preferred_element_type=F32)
        for row in range(i * step, (i + 1) * step):
            t_ref[pl.ds(order_ref[0, row], 1), :] = product_ref[row : row + 1, :]
    even, _, _ = position()
    width = near_ref.shape[0]
    to_right = size - width
    near_ref[...] = t_ref[pl.ds(pl.multiple_of(to_right * even, 8), width), :]
    far_ref[...] = t_ref[pl.ds(pl.multiple_of(to_right * (1 - even), 8), width), :]
    high, low = split(res_ref[...])
    b_high, b_low = split(basis_ref[...])
    both = jnp.concatenate([b_high, b_low], axis=0)
    first = jnp.dot(both, high, preferred_element_type=F32)
    second = jnp.dot(both, low, preferred_element_type=F32)
    half = basis_ref.shape[0]
    q = (first[:half] + second[:half] + first[half:])[:CV_DEV]
    q_ref[...] = jnp.broadcast_to(q[None], q_ref.shape)


def first_kernel(order_ref, loads_ref, near_in_ref, far_in_ref, mats_in_ref, wide_ref, own_rows_ref,
                 inverse_ref, basis_ref,
                 res_ref, t_ref, near_ref, far_ref, q_ref, mats_ref, extent_ref, rows_ref,
                 ordered_ref, product_ref):
    cases = loads_ref.shape[-1]
    plane_rows = 3 * NY * NZ
    planes = loads_ref.shape[0] // plane_rows
    even = position()[0] == 1

    def beside(start, stop):
        near, far = near_in_ref[start:stop], far_in_ref[start:stop]
        return jnp.where(even, far, near), jnp.where(even, near, far)

    left, right = beside(0, plane_rows)
    res_ref[:plane_rows] = left
    res_ref[plane_rows : (planes + 1) * plane_rows] = loads_ref[...]
    res_ref[(planes + 1) * plane_rows :] = right
    products(order_ref, inverse_ref, basis_ref, ordered_ref, product_ref, res_ref, t_ref, near_ref, far_ref, q_ref)

    extent = extent_ref.shape[1]
    span = part_blocks(plane_rows)
    extent_ref[...] = jnp.zeros_like(extent_ref)
    rows_ref[...] = jnp.zeros_like(rows_ref)
    extent_ref[CV_DEV : 2 * CV_DEV] = wide_ref[...]
    rows_ref[CV_DEV : 2 * CV_DEV] = own_rows_ref[...]
    groups = group_count(plane_rows, rows_ref.shape[1])
    for i in range(groups):
        at = plane_rows + 8 * i
        if i < span:
            left, right = beside(at, at + CV_DEV)
            extent_ref[:CV_DEV, 128 * i : 128 * (i + 1)] = left
            start = extent - 128 * span + 128 * i
            extent_ref[2 * CV_DEV : 3 * CV_DEV, start : start + 128] = right
        if i * 128 < rows_ref.shape[1]:
            left, right = beside(at + CV_DEV, at + 2 * CV_DEV)
            rows_ref[:CV_DEV, 128 * i : 128 * (i + 1)] = left
            rows_ref[2 * CV_DEV : 3 * CV_DEV, 128 * i : 128 * (i + 1)] = right
    at = plane_rows + 8 * groups
    left, right = beside(at, at + 2)
    for plane in range(2):
        mats_ref[plane] = on_lanes(left[plane : plane + 1], mats_ref.shape)
        mats_ref[planes + 2 + plane] = on_lanes(right[plane : plane + 1], mats_ref.shape)
    for plane in range(planes):
        mats_ref[2 + plane] = on_lanes(mats_in_ref[plane : plane + 1], mats_ref.shape)


def correction(q_ref, rows_ref, extent_ref, t_ref, near_ref, far_ref, z_ref):
    plane_rows = 3 * NY * NZ
    width = near_ref.shape[0] // plane_rows
    out_planes = t_ref.shape[0] // plane_rows + 2
    coarse = jnp.dot(rows_ref[...], q_ref[...], precision=lax.Precision.HIGHEST, preferred_element_type=F32)
    c_high, c_low = split(coarse)
    e_high, e_low = split(extent_ref[...])
    spread = lax.dot_general(
        jnp.concatenate([e_high, e_low, e_high], axis=0),
        jnp.concatenate([c_high, c_high, c_low], axis=0),
        (((0,), (0,)), ((), ())),
        preferred_element_type=F32,
    )
    even, has_left, has_right = position()
    even = even == 1

    def rows_at(ref, plane):
        return ref[plane * plane_rows : (plane + 1) * plane_rows]

    for plane in range(3 - width, out_planes - 3 + width):
        value = spread[plane * plane_rows : (plane + 1) * plane_rows]
        if 1 <= plane < out_planes - 1:
            value = value + rows_at(t_ref, plane - 1)
        if plane < 3:
            at = plane - (3 - width)
            value = value + jnp.where(even, rows_at(far_ref, at), rows_at(near_ref, at))
        if plane >= out_planes - 3:
            at = plane - (out_planes - 3)
            value = value + jnp.where(even, rows_at(near_ref, at), rows_at(far_ref, at))
        if plane < 2:
            value = value * has_left
        if plane >= out_planes - 2:
            value = value * has_right
        z_ref[plane] = node_grid(value)
    return coarse


def middle_kernel(with_solution, order_ref, q_in_ref, rows_ref, extent_ref, mats_ref, t_in_ref, near_in_ref,
                  far_in_ref, res_in_ref, *rest):
    if with_solution:
        solution_in_ref, *rest = rest
    inverse_ref, basis_ref, solution_ref, res_ref, t_ref, near_ref, far_ref, q_ref, z_ref, *scratch = rest
    correction(q_in_ref, rows_ref, extent_ref, t_in_ref, near_in_ref, far_in_ref, z_ref)
    _, has_left, has_right = position()
    window = z_ref.shape[0] - 2
    for plane in range(1, window + 1):
        applied = stencil_plane(mats_ref, plane, lambda p, c: z_ref[p, c])
        for component in range(3):
            at = block(plane - 1, component)
            value = res_in_ref[at] - RELAXATION * applied[component].reshape(NY * NZ, res_ref.shape[1])
            if plane == 1:
                value = value * has_left
            if plane == window:
                value = value * has_right
            res_ref[at] = value
    own = RELAXATION * z_ref[2:window].reshape(solution_ref.shape)
    solution_ref[...] = solution_in_ref[...] + own if with_solution else own
    products(order_ref, inverse_ref, basis_ref, *scratch, res_ref, t_ref, near_ref, far_ref, q_ref)


def last_kernel(q_in_ref, rows_ref, extent_ref, mats_ref, t_in_ref, near_in_ref, far_in_ref, res_in_ref,
                solution_in_ref, solution_ref, residual_ref, coarse_ref, z_ref):
    coarse = correction(q_in_ref, rows_ref, extent_ref, t_in_ref, near_in_ref, far_in_ref, z_ref)
    coarse_ref[...] = coarse[CV_DEV : 2 * CV_DEV]
    planes = z_ref.shape[0] - 4
    solution_ref[...] = solution_in_ref[...] + RELAXATION * z_ref[2 : planes + 2].reshape(solution_ref.shape)
    for plane in range(2, planes + 2):
        applied = stencil_plane(mats_ref, plane, lambda p, c: z_ref[p, c])
        for component in range(3):
            residual_ref[block(plane - 2, component)] = res_in_ref[
                block(plane - 1, component)
            ] - RELAXATION * applied[component].reshape(NY * NZ, residual_ref.shape[1])


def body(
    applied_loads,
    labels,
    shear_modulus,
    stiff_ratio,
    local_order,
    local_inverse,
    coarse_basis,
    coarse_inverse,
):
    planes, components, nodes, cases = applied_loads.shape
    window = planes + 2
    plane_rows = components * nodes
    size = window * plane_rows
    coarse_order = coarse_inverse.shape[1]
    count = lax.axis_size(AXES)
    near_pairs, far_pairs = swap_pairs(count)
    basis = coarse_basis[0]
    basis_pad = jnp.pad(basis, ((0, 16 - CV_DEV), (0, 0)))
    extent = size + 2 * plane_rows

    packed = jax.ShapeDtypeStruct((plane_rows + 8 * group_count(plane_rows, coarse_order) + 8, cases), F32)
    near_out, far_out, mats_own, own_rows, wide = pl.pallas_call(
        pack_kernel,
        out_shape=[
            packed,
            packed,
            jax.ShapeDtypeStruct((planes, 2 * nodes), F32),
            jax.ShapeDtypeStruct((CV_DEV, coarse_order), F32),
            jax.ShapeDtypeStruct((CV_DEV, extent), F32),
        ],
        in_specs=[HBM] * 6,
        out_specs=[VMEM] * 5,
        scratch_shapes=[
            pltpu.VMEM((1, shear_modulus.shape[0]), F32),
            pltpu.VMEM((1, shear_modulus.shape[0]), F32),
            pltpu.VMEM((components, nodes, cases), F32),
            pltpu.VMEM((components, nodes, cases), F32),
            pltpu.VMEM((planes, nodes), jnp.int32),
            pltpu.VMEM((CV_DEV, size), F32),
            pltpu.VMEM(coarse_inverse.shape, F32),
            pltpu.SemaphoreType.DMA((7,)),
        ],
        compiler_params=WHOLE,
    )(shear_modulus[None], stiff_ratio[None], applied_loads, labels, basis, coarse_inverse)
    near_in = lax.ppermute(near_out, AXES, near_pairs)
    far_in = lax.ppermute(far_out, AXES, far_pairs)

    def field(depth):
        return jax.ShapeDtypeStruct((depth * plane_rows, cases), F32)

    q_shape = jax.ShapeDtypeStruct((count, CV_DEV, cases), F32)
    cost = pl.CostEstimate(flops=2 * size * size * cases, bytes_accessed=2 * size * size, transcendentals=0)
    z_scratch = pltpu.VMEM((planes + 4, components, NY, NZ, cases), F32)
    scratch = [pltpu.VMEM((size, cases), F32), pltpu.VMEM((size, cases), F32)]
    loads = applied_loads.reshape(planes * plane_rows, cases)

    def move(near_out, far_out, q):
        near_in = lax.ppermute(near_out, AXES, near_pairs)
        far_in = lax.ppermute(far_out, AXES, far_pairs)
        q_all = lax.all_to_all(q, AXES, 0, 0).reshape(count * CV_DEV, cases)
        return near_in, far_in, q_all

    inverse = pl.pallas_call(
        stage_kernel,
        out_shape=jax.ShapeDtypeStruct((size, size), BF16),
        in_specs=[HBM],
        out_specs=VMEM,
        scratch_shapes=[pltpu.SemaphoreType.DMA((3,))],
        compiler_params=STAGE,
        cost_estimate=pl.CostEstimate(flops=4 * size**3, bytes_accessed=4 * size * size, transcendentals=0),
    )(local_inverse[0])
    res, t, near_out, far_out, q, mats_all, extents, inverse_rows = pl.pallas_call(
        first_kernel,
        out_shape=[
            field(window),
            field(window),
            field(3),
            field(3),
            q_shape,
            jax.ShapeDtypeStruct((planes + 4, 2, NY, NZ, cases), F32),
            jax.ShapeDtypeStruct((16, extent), F32),
            jax.ShapeDtypeStruct((16, coarse_order), F32),
        ],
        in_specs=[SMEM] + [VMEM] * 8,
        out_specs=[VMEM] * 8,
        scratch_shapes=scratch,
        compiler_params=PARAMS,
        cost_estimate=cost,
    )(local_order, loads, near_in, far_in, mats_own, wide, own_rows, inverse, basis_pad)
    near_in, far_in, q_all = move(near_out, far_out, q)
    solution = None
    for iteration in range(1, ITERS):
        width = 2 if iteration == ITERS - 1 else 3
        extra = [] if solution is None else [solution]
        operands = [local_order, q_all, inverse_rows, extents, mats_all, t, near_in, far_in, res, *extra,
                    inverse, basis_pad]
        solution, res, t, near_out, far_out, q = pl.pallas_call(
            functools.partial(middle_kernel, bool(extra)),
            out_shape=[field(planes), field(window), field(window), field(width), field(width), q_shape],
            in_specs=[SMEM] + [VMEM] * (len(operands) - 1),
            out_specs=[VMEM] * 6,
            scratch_shapes=[z_scratch, *scratch],
            compiler_params=PARAMS,
            cost_estimate=cost,
        )(*operands)
        near_in, far_in, q_all = move(near_out, far_out, q)
    solution, residual, coarse_values = pl.pallas_call(
        last_kernel,
        out_shape=[field(planes), field(planes), jax.ShapeDtypeStruct((CV_DEV, cases), F32)],
        in_specs=[VMEM] * 9,
        out_specs=[VMEM] * 3,
        scratch_shapes=[z_scratch],
        compiler_params=PARAMS,
    )(q_all, inverse_rows, extents, mats_all, t, near_in, far_in, res, solution)
    return (
        solution.reshape(planes, components, nodes, cases),
        residual.reshape(planes, components, nodes, cases),
        coarse_values,
    )


def solution(mesh):
    return jax.shard_map(
        body,
        mesh=mesh,
        in_specs=(
            P(("sub", "grp"), None, None, None),
            P(("sub", "grp"), None),
            P(),
            P(),
            P(("sub", "grp"), None),
            P(("sub", "grp"), None, None),
            P(("sub", "grp"), None, None),
            P("sub", None),
        ),
        out_specs=(
            P(("sub", "grp"), None, None, None),
            P(("sub", "grp"), None, None, None),
            P(("sub", "grp"), None),
        ),
        check_vma=False,
    )
```

```python
import functools

import jax
import jax.numpy as jnp
from jax import lax
from jax.experimental import pallas as pl
from jax.experimental.pallas import tpu as pltpu
from jax.sharding import PartitionSpec as P

NY = 8
NZ = 8
CV_DEV = 4
ITERS = 3
RELAXATION = 0.5
AXES = ("sub", "grp")
F32 = jnp.float32
BF16 = jnp.bfloat16
VMEM = pl.BlockSpec(memory_space=pltpu.VMEM)
HBM = pl.BlockSpec(memory_space=pltpu.HBM)
SMEM = pl.BlockSpec(memory_space=pltpu.SMEM)
PARAMS = pltpu.CompilerParams(vmem_limit_bytes=24 * 1024 * 1024)
STAGE = pltpu.CompilerParams(vmem_limit_bytes=50 * 1024 * 1024)
WHOLE = pltpu.CompilerParams(vmem_limit_bytes=56 * 1024 * 1024)


def position():
    place = lax.axis_index(AXES)
    even = 1 - lax.rem(place, 2)
    has_left = (place > 0).astype(F32)
    has_right = (place < lax.axis_size(AXES) - 1).astype(F32)
    return even, has_left, has_right


def swap_pairs(count):
    near = [(i, i ^ 1) for i in range(count)]
    far = []
    for i in range(1, count - 1, 2):
        far += [(i, i + 1), (i + 1, i)]
    return near, far


def pack_kernel(shear_hbm, ratio_hbm, labels_hbm, basis_hbm, coarse_hbm,
                near_ref, far_ref, mats_ref, rows_ref, wide_ref,
                shear_ref, ratio_ref, labels_ref, basis_ref, coarse_ref, sems):
    planes, nodes = labels_ref.shape
    plane_rows = 3 * NY * NZ
    moves = [
        (labels_hbm, labels_ref),
        (shear_hbm, shear_ref),
        (ratio_hbm, ratio_ref),
        (basis_hbm, basis_ref),
        (coarse_hbm, coarse_ref),
    ]
    copies = [pltpu.make_async_copy(source, target, sems.at[i]) for i, (source, target) in enumerate(moves)]
    for copy in copies:
        copy.start()
    even = position()[0] == 1
    wide_ref[...] = jnp.zeros_like(wide_ref)
    for copy in copies:
        copy.wait()
    labels = labels_ref[...]
    shear = jnp.zeros((planes, nodes), F32)
    normal = jnp.zeros((planes, nodes), F32)
    for region in range(shear_ref.shape[1]):
        value = shear_ref[:, region : region + 1]
        here = labels == region
        shear = jnp.where(here, value, shear)
        normal = jnp.where(here, value * (2.0 + ratio_ref[:, region : region + 1]), normal)
    both = jnp.concatenate([shear, normal], axis=1)
    mats_ref[...] = both
    mats_l, mats_r = both[:2], both[planes - 2 :]
    groups = group_count(plane_rows, coarse_ref.shape[1])
    near_ref[8 * groups : 8 * groups + 2] = jnp.where(even, mats_r, mats_l)
    far_ref[8 * groups : 8 * groups + 2] = jnp.where(even, mats_l, mats_r)
    near_ref[8 * groups + 2 :] = jnp.zeros_like(near_ref[8 * groups + 2 :])
    far_ref[8 * groups + 2 :] = jnp.zeros_like(far_ref[8 * groups + 2 :])
    wide_ref[:, plane_rows : plane_rows + basis_ref.shape[1]] = basis_ref[...]
    rows = coarse_ref[:CV_DEV]
    for member in range(1, coarse_ref.shape[0] // CV_DEV):
        rows = jnp.where(lax.axis_index("grp") == member, coarse_ref[member * CV_DEV : (member + 1) * CV_DEV], rows)
    rows_ref[...] = rows
    span = part_blocks(plane_rows)
    start_r = planes * plane_rows
    start_l = 4 * plane_rows - 128 * span
    nothing = jnp.zeros((CV_DEV, 128), F32)
    for i in range(groups):
        at = 8 * i
        block_l = block_r = row = nothing
        if i < span:
            block_l = wide_ref[:, start_l + 128 * i : start_l + 128 * (i + 1)]
            block_r = wide_ref[:, start_r + 128 * i : start_r + 128 * (i + 1)]
        if i * 128 < coarse_ref.shape[1]:
            row = rows[:, 128 * i : 128 * (i + 1)]
        near_ref[at : at + CV_DEV] = jnp.where(even, block_r, block_l)
        far_ref[at : at + CV_DEV] = jnp.where(even, block_l, block_r)
        near_ref[at + CV_DEV : at + 2 * CV_DEV] = row
        far_ref[at + CV_DEV : at + 2 * CV_DEV] = row


def stage_kernel(inverse_hbm, inverse_ref, sems):
    step = inverse_ref.shape[0] // 3
    copies = []
    for i in range(3):
        part = pl.ds(i * step, step)
        copies.append(pltpu.make_async_copy(inverse_hbm.at[part, :], inverse_ref.at[part, :], sems.at[i]))
    for copy in copies:
        copy.start()
    for copy in copies:
        copy.wait()


def on_lanes(row, shape):
    return jnp.transpose(jnp.broadcast_to(row, (shape[-1], row.shape[1]))).reshape(shape[1:])


def part_blocks(plane_rows):
    return -(-3 * plane_rows // 128)


def group_count(plane_rows, coarse_order):
    return max(part_blocks(plane_rows), coarse_order // 128)


def up_a(u):
    return jnp.concatenate([u[1:], jnp.zeros_like(u[:1])], axis=0)


def down_a(u):
    return jnp.concatenate([jnp.zeros_like(u[:1]), u[:-1]], axis=0)


def up_b(u):
    return pltpu.roll(u, NZ - 1, 1)


def down_b(u):
    return pltpu.roll(u, 1, 1)


def stencil_plane(mats, plane, field):
    b = lax.broadcasted_iota(jnp.int32, (NY, NZ, mats.shape[-1]), 1)
    last, first = b == NZ - 1, b == 0
    near_a, near_b_up, near_b_down, along, diagonal = [], [], [], [], []
    for kind in range(2):
        s = mats[plane, kind]
        half = 0.5 * s
        k_up = 0.5 * up_a(s) + half
        k_down = 0.5 * down_a(s) + half
        b_up = jnp.where(last, 0.0, 0.5 * up_b(s) + half)
        b_down = jnp.where(first, 0.0, 0.5 * down_b(s) + half)
        p_up = 0.5 * mats[plane + 1, kind] + half
        p_down = 0.5 * mats[plane - 1, kind] + half
        near_a.append((k_up, k_down))
        near_b_up.append(b_up)
        near_b_down.append(b_down)
        along.append((p_up, p_down))
        edge = jnp.where(last | first, half, 0.0)
        diagonal.append((p_up + p_down, k_up + k_down, b_up + b_down + edge))
    results = []
    for component in range(3):
        kinds = [1 if dimension == component else 0 for dimension in range(3)]
        u = field(plane, component)
        total = (diagonal[kinds[0]][0] + diagonal[kinds[1]][1] + diagonal[kinds[2]][2]) * u
        total = total - along[kinds[0]][0] * field(plane + 1, component)
        total = total - along[kinds[0]][1] * field(plane - 1, component)
        total = total - near_a[kinds[1]][0] * up_a(u)
        total = total - near_a[kinds[1]][1] * down_a(u)
        total = total - near_b_up[kinds[2]] * up_b(u)
        total = total - near_b_down[kinds[2]] * down_b(u)
        results.append(total)
    return results


def split(x):
    high = x.astype(BF16)
    return high, (x - high.astype(F32)).astype(BF16)


def block(plane, component):
    start = (plane * 3 + component) * NY * NZ
    return slice(start, start + NY * NZ)


def node_grid(rows):
    return rows.reshape(rows.shape[0] // (NY * NZ), NY, NZ, rows.shape[1])


def products(width, order_ref, inverse_ref, basis_ref, ordered_ref, product_ref, res_ref, t_ref, near_ref, far_ref,
             q_ref):
    size = res_ref.shape[0]
    for row in range(size):
        ordered_ref[row : row + 1, :] = res_ref[pl.ds(order_ref[0, row], 1), :]
    ordered = ordered_ref[...].astype(BF16)
    step = size // 3
    for i in range(3):
        part = slice(i * step, (i + 1) * step)
        product_ref[part, :] = jnp.dot(inverse_ref[part, :], ordered, preferred_element_type=F32)
        for row in range(i * step, (i + 1) * step):
            t_ref[pl.ds(order_ref[0, row], 1), :] = product_ref[row : row + 1, :]
    even, _, _ = position()
    to_right = size - width
    near_ref[:width] = t_ref[pl.ds(pl.multiple_of(to_right * even, 8), width), :]
    far_ref[:width] = t_ref[pl.ds(pl.multiple_of(to_right * (1 - even), 8), width), :]
    high, low = split(res_ref[...])
    b_high, b_low = split(basis_ref[...])
    both = jnp.concatenate([b_high, b_low], axis=0)
    first = jnp.dot(both, high, preferred_element_type=F32)
    second = jnp.dot(both, low, preferred_element_type=F32)
    half = basis_ref.shape[0]
    q = (first[:half] + second[:half] + first[half:])[:CV_DEV]
    q_ref[...] = jnp.broadcast_to(q[None], q_ref.shape)


def first_kernel(order_ref, loads_ref, near_in_ref, far_in_ref, near_pack_ref, far_pack_ref, inverse_ref, basis_ref,
                 res_ref, t_ref, near_ref, far_ref, q_ref, ordered_ref, product_ref):
    plane_rows = 3 * NY * NZ
    planes = loads_ref.shape[0] // plane_rows
    even = position()[0] == 1
    near, far = near_in_ref[...], far_in_ref[...]
    res_ref[:plane_rows] = jnp.where(even, far, near)
    res_ref[plane_rows : (planes + 1) * plane_rows] = loads_ref[...]
    res_ref[(planes + 1) * plane_rows :] = jnp.where(even, near, far)
    near_ref[3 * plane_rows :] = near_pack_ref[...]
    far_ref[3 * plane_rows :] = far_pack_ref[...]
    products(3 * plane_rows, order_ref, inverse_ref, basis_ref, ordered_ref, product_ref, res_ref, t_ref, near_ref,
             far_ref, q_ref)


def unpack(near_in_ref, far_in_ref, mats_in_ref, wide_ref, own_rows_ref, mats_ref, extent_ref, rows_ref):
    plane_rows = 3 * NY * NZ
    even = position()[0] == 1

    def beside(start, stop):
        start, stop = 3 * plane_rows + start, 3 * plane_rows + stop
        near, far = near_in_ref[start:stop], far_in_ref[start:stop]
        return jnp.where(even, far, near), jnp.where(even, near, far)

    extent = extent_ref.shape[1]
    span = part_blocks(plane_rows)
    extent_ref[...] = jnp.zeros_like(extent_ref)
    rows_ref[...] = jnp.zeros_like(rows_ref)
    extent_ref[CV_DEV : 2 * CV_DEV] = wide_ref[...]
    rows_ref[CV_DEV : 2 * CV_DEV] = own_rows_ref[...]
    groups = group_count(plane_rows, rows_ref.shape[1])
    for i in range(groups):
        at = 8 * i
        if i < span:
            left, right = beside(at, at + CV_DEV)
            extent_ref[:CV_DEV, 128 * i : 128 * (i + 1)] = left
            start = extent - 128 * span + 128 * i
            extent_ref[2 * CV_DEV : 3 * CV_DEV, start : start + 128] = right
        if i * 128 < rows_ref.shape[1]:
            left, right = beside(at + CV_DEV, at + 2 * CV_DEV)
            rows_ref[:CV_DEV, 128 * i : 128 * (i + 1)] = left
            rows_ref[2 * CV_DEV : 3 * CV_DEV, 128 * i : 128 * (i + 1)] = right
    left, right = beside(8 * groups, 8 * groups + 2)
    planes = mats_in_ref.shape[0]
    for plane in range(2):
        mats_ref[plane] = on_lanes(left[plane : plane + 1], mats_ref.shape)
        mats_ref[planes + 2 + plane] = on_lanes(right[plane : plane + 1], mats_ref.shape)
    for plane in range(planes):
        mats_ref[2 + plane] = on_lanes(mats_in_ref[plane : plane + 1], mats_ref.shape)


def correction(width, q_ref, rows_ref, extent_ref, t_ref, near_ref, far_ref, z_ref):
    plane_rows = 3 * NY * NZ
    out_planes = t_ref.shape[0] // plane_rows + 2
    coarse = jnp.dot(rows_ref[...], q_ref[...], precision=lax.Precision.HIGHEST, preferred_element_type=F32)
    c_high, c_low = split(coarse)
    e_high, e_low = split(extent_ref[...])
    spread = lax.dot_general(
        jnp.concatenate([e_high, e_low, e_high], axis=0),
        jnp.concatenate([c_high, c_high, c_low], axis=0),
        (((0,), (0,)), ((), ())),
        preferred_element_type=F32,
    )
    even, has_left, has_right = position()
    even = even == 1

    def rows_at(ref, plane):
        return ref[plane * plane_rows : (plane + 1) * plane_rows]

    for plane in range(3 - width, out_planes - 3 + width):
        value = spread[plane * plane_rows : (plane + 1) * plane_rows]
        if 1 <= plane < out_planes - 1:
            value = value + rows_at(t_ref, plane - 1)
        if plane < 3:
            at = plane - (3 - width)
            value = value + jnp.where(even, rows_at(far_ref, at), rows_at(near_ref, at))
        if plane >= out_planes - 3:
            at = plane - (out_planes - 3)
            value = value + jnp.where(even, rows_at(near_ref, at), rows_at(far_ref, at))
        if plane < 2:
            value = value * has_left
        if plane >= out_planes - 2:
            value = value * has_right
        z_ref[plane] = node_grid(value)
    return coarse


def second_kernel(width, order_ref, q_in_ref, mats_in_ref, wide_ref, own_rows_ref, t_in_ref, near_in_ref, far_in_ref,
                  res_in_ref, inverse_ref, basis_ref, solution_ref, res_ref, t_ref, near_ref, far_ref, q_ref,
                  mats_ref, extent_ref, rows_ref, *scratch):
    unpack(near_in_ref, far_in_ref, mats_in_ref, wide_ref, own_rows_ref, mats_ref, extent_ref, rows_ref)
    middle_kernel(width, order_ref, q_in_ref, rows_ref, extent_ref, mats_ref, t_in_ref, near_in_ref, far_in_ref,
                  res_in_ref, None, inverse_ref, basis_ref, solution_ref, res_ref, t_ref, near_ref, far_ref, q_ref,
                  *scratch)


def middle_kernel(width, order_ref, q_in_ref, rows_ref, extent_ref, mats_ref, t_in_ref, near_in_ref, far_in_ref,
                  res_in_ref, solution_in_ref, inverse_ref, basis_ref, solution_ref, res_ref, t_ref, near_ref,
                  far_ref, q_ref, z_ref, *scratch):
    correction(3, q_in_ref, rows_ref, extent_ref, t_in_ref, near_in_ref, far_in_ref, z_ref)
    _, has_left, has_right = position()
    window = z_ref.shape[0] - 2
    for plane in range(1, window + 1):
        applied = stencil_plane(mats_ref, plane, lambda p, c: z_ref[p, c])
        for component in range(3):
            at = block(plane - 1, component)
            value = res_in_ref[at] - RELAXATION * applied[component].reshape(NY * NZ, res_ref.shape[1])
            if plane == 1:
                value = value * has_left
            if plane == window:
                value = value * has_right
            res_ref[at] = value
    own = RELAXATION * z_ref[2:window].reshape(solution_ref.shape)
    solution_ref[...] = own if solution_in_ref is None else solution_in_ref[...] + own
    products(width * 3 * NY * NZ, order_ref, inverse_ref, basis_ref, *scratch, res_ref, t_ref, near_ref, far_ref, q_ref)


def last_kernel(q_in_ref, rows_ref, extent_ref, mats_ref, t_in_ref, near_in_ref, far_in_ref, res_in_ref,
                solution_in_ref, solution_ref, residual_ref, coarse_ref, z_ref):
    coarse = correction(2, q_in_ref, rows_ref, extent_ref, t_in_ref, near_in_ref, far_in_ref, z_ref)
    coarse_ref[...] = coarse[CV_DEV : 2 * CV_DEV]
    planes = z_ref.shape[0] - 4
    solution_ref[...] = solution_in_ref[...] + RELAXATION * z_ref[2 : planes + 2].reshape(solution_ref.shape)
    for plane in range(2, planes + 2):
        applied = stencil_plane(mats_ref, plane, lambda p, c: z_ref[p, c])
        for component in range(3):
            residual_ref[block(plane - 2, component)] = res_in_ref[
                block(plane - 1, component)
            ] - RELAXATION * applied[component].reshape(NY * NZ, residual_ref.shape[1])


def body(
    applied_loads,
    labels,
    shear_modulus,
    stiff_ratio,
    local_order,
    local_inverse,
    coarse_basis,
    coarse_inverse,
):
    planes, components, nodes, cases = applied_loads.shape
    window = planes + 2
    plane_rows = components * nodes
    size = window * plane_rows
    coarse_order = coarse_inverse.shape[1]
    count = lax.axis_size(AXES)
    near_pairs, far_pairs = swap_pairs(count)
    basis = coarse_basis[0]
    basis_pad = jnp.pad(basis, ((0, 16 - CV_DEV), (0, 0)))
    extent = size + 2 * plane_rows

    even = 1 - lax.rem(lax.axis_index(AXES), 2)

    def loads_plane(plane):
        return lax.dynamic_index_in_dim(applied_loads, plane, 0, keepdims=False).reshape(plane_rows, cases)

    near_in = lax.ppermute(loads_plane((planes - 1) * even), AXES, near_pairs)
    far_in = lax.ppermute(loads_plane((planes - 1) * (1 - even)), AXES, far_pairs)

    pack_rows = 8 * group_count(plane_rows, coarse_order) + 8
    packed = jax.ShapeDtypeStruct((pack_rows, cases), F32)
    near_pack, far_pack, mats_own, own_rows, wide = pl.pallas_call(
        pack_kernel,
        out_shape=[
            packed,
            packed,
            jax.ShapeDtypeStruct((planes, 2 * nodes), F32),
            jax.ShapeDtypeStruct((CV_DEV, coarse_order), F32),
            jax.ShapeDtypeStruct((CV_DEV, extent), F32),
        ],
        in_specs=[HBM] * 5,
        out_specs=[VMEM] * 5,
        scratch_shapes=[
            pltpu.VMEM((1, shear_modulus.shape[0]), F32),
            pltpu.VMEM((1, shear_modulus.shape[0]), F32),
            pltpu.VMEM((planes, nodes), jnp.int32),
            pltpu.VMEM((CV_DEV, size), F32),
            pltpu.VMEM(coarse_inverse.shape, F32),
            pltpu.SemaphoreType.DMA((5,)),
        ],
        compiler_params=WHOLE,
        cost_estimate=pl.CostEstimate(flops=8 * size**3, bytes_accessed=4 * size * size, transcendentals=0),
    )(shear_modulus[None], stiff_ratio[None], labels, basis, coarse_inverse)

    def field(depth):
        return jax.ShapeDtypeStruct((depth * plane_rows, cases), F32)

    q_shape = jax.ShapeDtypeStruct((count, CV_DEV, cases), F32)
    cost = pl.CostEstimate(flops=2 * size * size * cases, bytes_accessed=2 * size * size, transcendentals=0)
    z_scratch = pltpu.VMEM((planes + 4, components, NY, NZ, cases), F32)
    scratch = [pltpu.VMEM((size, cases), F32), pltpu.VMEM((size, cases), F32)]
    loads = applied_loads.reshape(planes * plane_rows, cases)

    def move(near_out, far_out, q):
        near_in = lax.ppermute(near_out, AXES, near_pairs)
        far_in = lax.ppermute(far_out, AXES, far_pairs)
        q_all = lax.all_to_all(q, AXES, 0, 0).reshape(count * CV_DEV, cases)
        return near_in, far_in, q_all

    inverse = pl.pallas_call(
        stage_kernel,
        out_shape=jax.ShapeDtypeStruct((size, size), BF16),
        in_specs=[HBM],
        out_specs=VMEM,
        scratch_shapes=[pltpu.SemaphoreType.DMA((3,))],
        compiler_params=STAGE,
        cost_estimate=pl.CostEstimate(flops=4 * size**3, bytes_accessed=4 * size * size, transcendentals=0),
    )(local_inverse[0])
    carried = jax.ShapeDtypeStruct((3 * plane_rows + pack_rows, cases), F32)
    res, t, near_out, far_out, q = pl.pallas_call(
        first_kernel,
        out_shape=[field(window), field(window), carried, carried, q_shape],
        in_specs=[SMEM] + [VMEM] * 7,
        out_specs=[VMEM] * 5,
        scratch_shapes=scratch,
        compiler_params=PARAMS,
        cost_estimate=cost,
    )(local_order, loads, near_in, far_in, near_pack, far_pack, inverse, basis_pad)
    near_in, far_in, q_all = move(near_out, far_out, q)
    for iteration in range(1, ITERS):
        width = 2 if iteration == ITERS - 1 else 3
        outs = [field(planes), field(window), field(window), field(width), field(width), q_shape]
        if iteration == 1:
            kernel = second_kernel
            operands = [local_order, q_all, mats_own, wide, own_rows, t, near_in, far_in, res, inverse, basis_pad]
            outs += [
                jax.ShapeDtypeStruct((planes + 4, 2, NY, NZ, cases), F32),
                jax.ShapeDtypeStruct((16, extent), F32),
                jax.ShapeDtypeStruct((16, coarse_order), F32),
            ]
        else:
            kernel = middle_kernel
            operands = [local_order, q_all, inverse_rows, extents, mats_all, t, near_in, far_in, res, solution,
                        inverse, basis_pad]
        solution, res, t, near_out, far_out, q, *setup = pl.pallas_call(
            functools.partial(kernel, width),
            out_shape=outs,
            in_specs=[SMEM] + [VMEM] * (len(operands) - 1),
            out_specs=[VMEM] * len(outs),
            scratch_shapes=[z_scratch, *scratch],
            compiler_params=PARAMS,
            cost_estimate=cost,
        )(*operands)
        if setup:
            mats_all, extents, inverse_rows = setup
        near_in, far_in, q_all = move(near_out, far_out, q)
    solution, residual, coarse_values = pl.pallas_call(
        last_kernel,
        out_shape=[field(planes), field(planes), jax.ShapeDtypeStruct((CV_DEV, cases), F32)],
        in_specs=[VMEM] * 9,
        out_specs=[VMEM] * 3,
        scratch_shapes=[z_scratch],
        compiler_params=PARAMS,
    )(q_all, inverse_rows, extents, mats_all, t, near_in, far_in, res, solution)
    return (
        solution.reshape(planes, components, nodes, cases),
        residual.reshape(planes, components, nodes, cases),
        coarse_values,
    )


def solution(mesh):
    return jax.shard_map(
        body,
        mesh=mesh,
        in_specs=(
            P(("sub", "grp"), None, None, None),
            P(("sub", "grp"), None),
            P(),
            P(),
            P(("sub", "grp"), None),
            P(("sub", "grp"), None, None),
            P(("sub", "grp"), None, None),
            P("sub", None),
        ),
        out_specs=(
            P(("sub", "grp"), None, None, None),
            P(("sub", "grp"), None, None, None),
            P(("sub", "grp"), None),
        ),
        check_vma=False,
    )
```

```python
import functools

import jax
import jax.numpy as jnp
from jax import lax
from jax.experimental import pallas as pl
from jax.experimental.pallas import tpu as pltpu
from jax.sharding import PartitionSpec as P

NY = 8
NZ = 8
CV_DEV = 4
ITERS = 3
RELAXATION = 0.5
AXES = ("sub", "grp")
F32 = jnp.float32
BF16 = jnp.bfloat16
VMEM = pl.BlockSpec(memory_space=pltpu.VMEM)
HBM = pl.BlockSpec(memory_space=pltpu.HBM)
SMEM = pl.BlockSpec(memory_space=pltpu.SMEM)
PARAMS = pltpu.CompilerParams(vmem_limit_bytes=24 * 1024 * 1024)
STAGE = pltpu.CompilerParams(vmem_limit_bytes=50 * 1024 * 1024)
WHOLE = pltpu.CompilerParams(vmem_limit_bytes=56 * 1024 * 1024)


def position():
    place = lax.axis_index(AXES)
    odd = lax.rem(place, 2)
    has_left = (place > 0).astype(F32)
    has_right = (place < lax.axis_size(AXES) - 1).astype(F32)
    return odd, has_left, has_right


def swap_pairs(count):
    near = [(i, i ^ 1) for i in range(count)]
    far = []
    for i in range(1, count - 1, 2):
        far += [(i, i + 1), (i + 1, i)]
    return near, far


def pack_kernel(shear_hbm, ratio_hbm, labels_hbm, basis_hbm, coarse_hbm,
                far_ref, near_ref, mats_ref, rows_ref, wide_ref,
                shear_ref, ratio_ref, labels_ref, basis_ref, coarse_ref, sems):
    planes, nodes = labels_ref.shape
    plane_rows = 3 * NY * NZ
    moves = [
        (labels_hbm, labels_ref),
        (shear_hbm, shear_ref),
        (ratio_hbm, ratio_ref),
        (basis_hbm, basis_ref),
        (coarse_hbm, coarse_ref),
    ]
    copies = [pltpu.make_async_copy(source, target, sems.at[i]) for i, (source, target) in enumerate(moves)]
    for copy in copies:
        copy.start()
    odd = position()[0] == 1
    wide_ref[...] = jnp.zeros_like(wide_ref)
    for copy in copies:
        copy.wait()
    labels = labels_ref[...]
    shear = jnp.zeros((planes, nodes), F32)
    normal = jnp.zeros((planes, nodes), F32)
    for region in range(shear_ref.shape[1]):
        value = shear_ref[:, region : region + 1]
        here = labels == region
        shear = jnp.where(here, value, shear)
        normal = jnp.where(here, value * (2.0 + ratio_ref[:, region : region + 1]), normal)
    both = jnp.concatenate([shear, normal], axis=1)
    mats_ref[...] = both
    mats_l, mats_r = both[:2], both[planes - 2 :]
    groups = group_count(plane_rows, coarse_ref.shape[1])
    far_ref[8 * groups : 8 * groups + 2] = jnp.where(odd, mats_r, mats_l)
    near_ref[8 * groups : 8 * groups + 2] = jnp.where(odd, mats_l, mats_r)
    far_ref[8 * groups + 2 :] = jnp.zeros_like(far_ref[8 * groups + 2 :])
    near_ref[8 * groups + 2 :] = jnp.zeros_like(near_ref[8 * groups + 2 :])
    wide_ref[:, plane_rows : plane_rows + basis_ref.shape[1]] = basis_ref[...]
    rows = coarse_ref[:CV_DEV]
    for member in range(1, coarse_ref.shape[0] // CV_DEV):
        rows = jnp.where(lax.axis_index("grp") == member, coarse_ref[member * CV_DEV : (member + 1) * CV_DEV], rows)
    rows_ref[...] = rows
    span = part_blocks(plane_rows)
    start_r = planes * plane_rows
    start_l = 4 * plane_rows - 128 * span
    nothing = jnp.zeros((CV_DEV, 128), F32)
    for i in range(groups):
        at = 8 * i
        block_l = block_r = row = nothing
        if i < span:
            block_l = wide_ref[:, start_l + 128 * i : start_l + 128 * (i + 1)]
            block_r = wide_ref[:, start_r + 128 * i : start_r + 128 * (i + 1)]
        if i * 128 < coarse_ref.shape[1]:
            row = rows[:, 128 * i : 128 * (i + 1)]
        far_ref[at : at + CV_DEV] = jnp.where(odd, block_r, block_l)
        near_ref[at : at + CV_DEV] = jnp.where(odd, block_l, block_r)
        far_ref[at + CV_DEV : at + 2 * CV_DEV] = row
        near_ref[at + CV_DEV : at + 2 * CV_DEV] = row


def stage_kernel(inverse_hbm, inverse_ref, sems):
    step = inverse_ref.shape[0] // 3
    copies = []
    for i in range(3):
        part = pl.ds(i * step, step)
        copies.append(pltpu.make_async_copy(inverse_hbm.at[part, :], inverse_ref.at[part, :], sems.at[i]))
    for copy in copies:
        copy.start()
    for copy in copies:
        copy.wait()


def on_lanes(row, shape):
    return jnp.transpose(jnp.broadcast_to(row, (shape[-1], row.shape[1]))).reshape(shape[1:])


def part_blocks(plane_rows):
    return -(-3 * plane_rows // 128)


def group_count(plane_rows, coarse_order):
    return max(part_blocks(plane_rows), coarse_order // 128)


def up_a(u):
    return jnp.concatenate([u[1:], jnp.zeros_like(u[:1])], axis=0)


def down_a(u):
    return jnp.concatenate([jnp.zeros_like(u[:1]), u[:-1]], axis=0)


def up_b(u):
    return pltpu.roll(u, NZ - 1, 1)


def down_b(u):
    return pltpu.roll(u, 1, 1)


def stencil_plane(mats, plane, field):
    b = lax.broadcasted_iota(jnp.int32, (NY, NZ, mats.shape[-1]), 1)
    last, first = b == NZ - 1, b == 0
    near_a, near_b_up, near_b_down, along, diagonal = [], [], [], [], []
    for kind in range(2):
        s = mats[plane, kind]
        half = 0.5 * s
        k_up = 0.5 * up_a(s) + half
        k_down = 0.5 * down_a(s) + half
        b_up = jnp.where(last, 0.0, 0.5 * up_b(s) + half)
        b_down = jnp.where(first, 0.0, 0.5 * down_b(s) + half)
        p_up = 0.5 * mats[plane + 1, kind] + half
        p_down = 0.5 * mats[plane - 1, kind] + half
        near_a.append((k_up, k_down))
        near_b_up.append(b_up)
        near_b_down.append(b_down)
        along.append((p_up, p_down))
        edge = jnp.where(last | first, half, 0.0)
        diagonal.append((p_up + p_down, k_up + k_down, b_up + b_down + edge))
    results = []
    for component in range(3):
        kinds = [1 if dimension == component else 0 for dimension in range(3)]
        u = field(plane, component)
        total = (diagonal[kinds[0]][0] + diagonal[kinds[1]][1] + diagonal[kinds[2]][2]) * u
        total = total - along[kinds[0]][0] * field(plane + 1, component)
        total = total - along[kinds[0]][1] * field(plane - 1, component)
        total = total - near_a[kinds[1]][0] * up_a(u)
        total = total - near_a[kinds[1]][1] * down_a(u)
        total = total - near_b_up[kinds[2]] * up_b(u)
        total = total - near_b_down[kinds[2]] * down_b(u)
        results.append(total)
    return results


def split(x):
    high = x.astype(BF16)
    return high, (x - high.astype(F32)).astype(BF16)


def block(plane, component):
    start = (plane * 3 + component) * NY * NZ
    return slice(start, start + NY * NZ)


def node_grid(rows):
    return rows.reshape(rows.shape[0] // (NY * NZ), NY, NZ, rows.shape[1])


def products(width, order_ref, inverse_ref, basis_ref, ordered_ref, product_ref, res_ref, t_ref, far_ref, near_ref,
             q_ref):
    size = res_ref.shape[0]
    for row in range(size):
        ordered_ref[row : row + 1, :] = res_ref[pl.ds(order_ref[0, row], 1), :]
    ordered = ordered_ref[...].astype(BF16)
    step = size // 3
    for i in range(3):
        part = slice(i * step, (i + 1) * step)
        product_ref[part, :] = jnp.dot(inverse_ref[part, :], ordered, preferred_element_type=F32)
        for row in range(i * step, (i + 1) * step):
            t_ref[pl.ds(order_ref[0, row], 1), :] = product_ref[row : row + 1, :]
    odd, _, _ = position()
    to_right = size - width
    far_ref[:width] = t_ref[pl.ds(pl.multiple_of(to_right * odd, 8), width), :]
    near_ref[:width] = t_ref[pl.ds(pl.multiple_of(to_right * (1 - odd), 8), width), :]
    high, low = split(res_ref[...])
    b_high, b_low = split(basis_ref[...])
    both = jnp.concatenate([b_high, b_low], axis=0)
    first = jnp.dot(both, high, preferred_element_type=F32)
    second = jnp.dot(both, low, preferred_element_type=F32)
    half = basis_ref.shape[0]
    q = (first[:half] + second[:half] + first[half:])[:CV_DEV]
    q_ref[...] = jnp.broadcast_to(q[None], q_ref.shape)


def first_kernel(order_ref, loads_ref, far_in_ref, near_in_ref, far_pack_ref, near_pack_ref, inverse_ref, basis_ref,
                 res_ref, t_ref, far_ref, near_ref, q_ref, ordered_ref, product_ref):
    plane_rows = 3 * NY * NZ
    planes = loads_ref.shape[0] // plane_rows
    odd = position()[0] == 1
    far, near = far_in_ref[...], near_in_ref[...]
    res_ref[:plane_rows] = jnp.where(odd, near, far)
    res_ref[plane_rows : (planes + 1) * plane_rows] = loads_ref[...]
    res_ref[(planes + 1) * plane_rows :] = jnp.where(odd, far, near)
    far_ref[3 * plane_rows :] = far_pack_ref[...]
    near_ref[3 * plane_rows :] = near_pack_ref[...]
    products(3 * plane_rows, order_ref, inverse_ref, basis_ref, ordered_ref, product_ref, res_ref, t_ref, far_ref,
             near_ref, q_ref)


def unpack(far_in_ref, near_in_ref, mats_in_ref, wide_ref, own_rows_ref, mats_ref, extent_ref, rows_ref):
    plane_rows = 3 * NY * NZ
    odd = position()[0] == 1

    def beside(start, stop):
        start, stop = 3 * plane_rows + start, 3 * plane_rows + stop
        far, near = far_in_ref[start:stop], near_in_ref[start:stop]
        return jnp.where(odd, near, far), jnp.where(odd, far, near)

    extent = extent_ref.shape[1]
    span = part_blocks(plane_rows)
    extent_ref[...] = jnp.zeros_like(extent_ref)
    rows_ref[...] = jnp.zeros_like(rows_ref)
    extent_ref[CV_DEV : 2 * CV_DEV] = wide_ref[...]
    rows_ref[CV_DEV : 2 * CV_DEV] = own_rows_ref[...]
    groups = group_count(plane_rows, rows_ref.shape[1])
    for i in range(groups):
        at = 8 * i
        if i < span:
            left, right = beside(at, at + CV_DEV)
            extent_ref[:CV_DEV, 128 * i : 128 * (i + 1)] = left
            start = extent - 128 * span + 128 * i
            extent_ref[2 * CV_DEV : 3 * CV_DEV, start : start + 128] = right
        if i * 128 < rows_ref.shape[1]:
            left, right = beside(at + CV_DEV, at + 2 * CV_DEV)
            rows_ref[:CV_DEV, 128 * i : 128 * (i + 1)] = left
            rows_ref[2 * CV_DEV : 3 * CV_DEV, 128 * i : 128 * (i + 1)] = right
    left, right = beside(8 * groups, 8 * groups + 2)
    planes = mats_in_ref.shape[0]
    for plane in range(2):
        mats_ref[plane] = on_lanes(left[plane : plane + 1], mats_ref.shape)
        mats_ref[planes + 2 + plane] = on_lanes(right[plane : plane + 1], mats_ref.shape)
    for plane in range(planes):
        mats_ref[2 + plane] = on_lanes(mats_in_ref[plane : plane + 1], mats_ref.shape)


def correction(width, q_ref, rows_ref, extent_ref, t_ref, far_ref, near_ref, z_ref):
    plane_rows = 3 * NY * NZ
    out_planes = t_ref.shape[0] // plane_rows + 2
    coarse = jnp.dot(rows_ref[...], q_ref[...], precision=lax.Precision.HIGHEST, preferred_element_type=F32)
    c_high, c_low = split(coarse)
    e_high, e_low = split(extent_ref[...])
    spread = lax.dot_general(
        jnp.concatenate([e_high, e_low, e_high], axis=0),
        jnp.concatenate([c_high, c_high, c_low], axis=0),
        (((0,), (0,)), ((), ())),
        preferred_element_type=F32,
    )
    odd, has_left, has_right = position()
    odd = odd == 1

    def rows_at(ref, plane):
        return ref[plane * plane_rows : (plane + 1) * plane_rows]

    for plane in range(3 - width, out_planes - 3 + width):
        value = spread[plane * plane_rows : (plane + 1) * plane_rows]
        if 1 <= plane < out_planes - 1:
            value = value + rows_at(t_ref, plane - 1)
        if plane < 3:
            at = plane - (3 - width)
            value = value + jnp.where(odd, rows_at(near_ref, at), rows_at(far_ref, at))
        if plane >= out_planes - 3:
            at = plane - (out_planes - 3)
            value = value + jnp.where(odd, rows_at(far_ref, at), rows_at(near_ref, at))
        if plane < 2:
            value = value * has_left
        if plane >= out_planes - 2:
            value = value * has_right
        z_ref[plane] = node_grid(value)
    return coarse


def second_kernel(width, order_ref, q_in_ref, mats_in_ref, wide_ref, own_rows_ref, t_in_ref, far_in_ref, near_in_ref,
                  res_in_ref, inverse_ref, basis_ref, solution_ref, res_ref, t_ref, far_ref, near_ref, q_ref,
                  mats_ref, extent_ref, rows_ref, *scratch):
    unpack(far_in_ref, near_in_ref, mats_in_ref, wide_ref, own_rows_ref, mats_ref, extent_ref, rows_ref)
    middle_kernel(width, order_ref, q_in_ref, rows_ref, extent_ref, mats_ref, t_in_ref, far_in_ref, near_in_ref,
                  res_in_ref, None, inverse_ref, basis_ref, solution_ref, res_ref, t_ref, far_ref, near_ref, q_ref,
                  *scratch)


def middle_kernel(width, order_ref, q_in_ref, rows_ref, extent_ref, mats_ref, t_in_ref, far_in_ref, near_in_ref,
                  res_in_ref, solution_in_ref, inverse_ref, basis_ref, solution_ref, res_ref, t_ref, far_ref,
                  near_ref, q_ref, z_ref, *scratch):
    correction(3, q_in_ref, rows_ref, extent_ref, t_in_ref, far_in_ref, near_in_ref, z_ref)
    _, has_left, has_right = position()
    window = z_ref.shape[0] - 2
    for plane in range(1, window + 1):
        applied = stencil_plane(mats_ref, plane, lambda p, c: z_ref[p, c])
        for component in range(3):
            at = block(plane - 1, component)
            value = res_in_ref[at] - RELAXATION * applied[component].reshape(NY * NZ, res_ref.shape[1])
            if plane == 1:
                value = value * has_left
            if plane == window:
                value = value * has_right
            res_ref[at] = value
    own = RELAXATION * z_ref[2:window].reshape(solution_ref.shape)
    solution_ref[...] = own if solution_in_ref is None else solution_in_ref[...] + own
    products(width * 3 * NY * NZ, order_ref, inverse_ref, basis_ref, *scratch, res_ref, t_ref, far_ref, near_ref, q_ref)


def last_kernel(q_in_ref, rows_ref, extent_ref, mats_ref, t_in_ref, far_in_ref, near_in_ref, res_in_ref,
                solution_in_ref, solution_ref, residual_ref, coarse_ref, z_ref):
    coarse = correction(2, q_in_ref, rows_ref, extent_ref, t_in_ref, far_in_ref, near_in_ref, z_ref)
    coarse_ref[...] = coarse[CV_DEV : 2 * CV_DEV]
    planes = z_ref.shape[0] - 4
    solution_ref[...] = solution_in_ref[...] + RELAXATION * z_ref[2 : planes + 2].reshape(solution_ref.shape)
    for plane in range(2, planes + 2):
        applied = stencil_plane(mats_ref, plane, lambda p, c: z_ref[p, c])
        for component in range(3):
            residual_ref[block(plane - 2, component)] = res_in_ref[
                block(plane - 1, component)
            ] - RELAXATION * applied[component].reshape(NY * NZ, residual_ref.shape[1])


def body(
    applied_loads,
    labels,
    shear_modulus,
    stiff_ratio,
    local_order,
    local_inverse,
    coarse_basis,
    coarse_inverse,
):
    planes, components, nodes, cases = applied_loads.shape
    window = planes + 2
    plane_rows = components * nodes
    size = window * plane_rows
    coarse_order = coarse_inverse.shape[1]
    count = lax.axis_size(AXES)
    near_pairs, far_pairs = swap_pairs(count)
    basis = coarse_basis[0]
    basis_pad = jnp.pad(basis, ((0, 16 - CV_DEV), (0, 0)))
    extent = size + 2 * plane_rows

    odd = lax.rem(lax.axis_index(AXES), 2)

    def loads_plane(plane):
        return lax.dynamic_index_in_dim(applied_loads, plane, 0, keepdims=False).reshape(plane_rows, cases)

    far_in = lax.ppermute(loads_plane((planes - 1) * odd), AXES, far_pairs)
    near_in = lax.ppermute(loads_plane((planes - 1) * (1 - odd)), AXES, near_pairs)

    pack_rows = 8 * group_count(plane_rows, coarse_order) + 8
    packed = jax.ShapeDtypeStruct((pack_rows, cases), F32)
    far_pack, near_pack, mats_own, own_rows, wide = pl.pallas_call(
        pack_kernel,
        out_shape=[
            packed,
            packed,
            jax.ShapeDtypeStruct((planes, 2 * nodes), F32),
            jax.ShapeDtypeStruct((CV_DEV, coarse_order), F32),
            jax.ShapeDtypeStruct((CV_DEV, extent), F32),
        ],
        in_specs=[HBM] * 5,
        out_specs=[VMEM] * 5,
        scratch_shapes=[
            pltpu.VMEM((1, shear_modulus.shape[0]), F32),
            pltpu.VMEM((1, shear_modulus.shape[0]), F32),
            pltpu.VMEM((planes, nodes), jnp.int32),
            pltpu.VMEM((CV_DEV, size), F32),
            pltpu.VMEM(coarse_inverse.shape, F32),
            pltpu.SemaphoreType.DMA((5,)),
        ],
        compiler_params=WHOLE,
        cost_estimate=pl.CostEstimate(flops=8 * size**3, bytes_accessed=4 * size * size, transcendentals=0),
    )(shear_modulus[None], stiff_ratio[None], labels, basis, coarse_inverse)

    def field(depth):
        return jax.ShapeDtypeStruct((depth * plane_rows, cases), F32)

    q_shape = jax.ShapeDtypeStruct((count, CV_DEV, cases), F32)
    cost = pl.CostEstimate(flops=2 * size * size * cases, bytes_accessed=2 * size * size, transcendentals=0)
    z_scratch = pltpu.VMEM((planes + 4, components, NY, NZ, cases), F32)
    scratch = [pltpu.VMEM((size, cases), F32), pltpu.VMEM((size, cases), F32)]
    loads = applied_loads.reshape(planes * plane_rows, cases)

    def move(far_out, near_out, q):
        far_in = lax.ppermute(far_out, AXES, far_pairs)
        near_in = lax.ppermute(near_out, AXES, near_pairs)
        q_all = lax.all_to_all(q, AXES, 0, 0).reshape(count * CV_DEV, cases)
        return far_in, near_in, q_all

    inverse = pl.pallas_call(
        stage_kernel,
        out_shape=jax.ShapeDtypeStruct((size, size), BF16),
        in_specs=[HBM],
        out_specs=VMEM,
        scratch_shapes=[pltpu.SemaphoreType.DMA((3,))],
        compiler_params=STAGE,
        cost_estimate=pl.CostEstimate(flops=4 * size**3, bytes_accessed=4 * size * size, transcendentals=0),
    )(local_inverse[0])
    carried = jax.ShapeDtypeStruct((3 * plane_rows + pack_rows, cases), F32)
    res, t, far_out, near_out, q = pl.pallas_call(
        first_kernel,
        out_shape=[field(window), field(window), carried, carried, q_shape],
        in_specs=[SMEM] + [VMEM] * 7,
        out_specs=[VMEM] * 5,
        scratch_shapes=scratch,
        compiler_params=PARAMS,
        cost_estimate=cost,
    )(local_order, loads, far_in, near_in, far_pack, near_pack, inverse, basis_pad)
    far_in, near_in, q_all = move(far_out, near_out, q)
    for iteration in range(1, ITERS):
        width = 2 if iteration == ITERS - 1 else 3
        outs = [field(planes), field(window), field(window), field(width), field(width), q_shape]
        if iteration == 1:
            kernel = second_kernel
            operands = [local_order, q_all, mats_own, wide, own_rows, t, far_in, near_in, res, inverse, basis_pad]
            outs += [
                jax.ShapeDtypeStruct((planes + 4, 2, NY, NZ, cases), F32),
                jax.ShapeDtypeStruct((16, extent), F32),
                jax.ShapeDtypeStruct((16, coarse_order), F32),
            ]
        else:
            kernel = middle_kernel
            operands = [local_order, q_all, inverse_rows, extents, mats_all, t, far_in, near_in, res, solution,
                        inverse, basis_pad]
        solution, res, t, far_out, near_out, q, *setup = pl.pallas_call(
            functools.partial(kernel, width),
            out_shape=outs,
            in_specs=[SMEM] + [VMEM] * (len(operands) - 1),
            out_specs=[VMEM] * len(outs),
            scratch_shapes=[z_scratch, *scratch],
            compiler_params=PARAMS,
            cost_estimate=cost,
        )(*operands)
        if setup:
            mats_all, extents, inverse_rows = setup
        far_in, near_in, q_all = move(far_out, near_out, q)
    solution, residual, coarse_values = pl.pallas_call(
        last_kernel,
        out_shape=[field(planes), field(planes), jax.ShapeDtypeStruct((CV_DEV, cases), F32)],
        in_specs=[VMEM] * 9,
        out_specs=[VMEM] * 3,
        scratch_shapes=[z_scratch],
        compiler_params=PARAMS,
    )(q_all, inverse_rows, extents, mats_all, t, far_in, near_in, res, solution)
    return (
        solution.reshape(planes, components, nodes, cases),
        residual.reshape(planes, components, nodes, cases),
        coarse_values,
    )


def solution(mesh):
    return jax.shard_map(
        body,
        mesh=mesh,
        in_specs=(
            P(("sub", "grp"), None, None, None),
            P(("sub", "grp"), None),
            P(),
            P(),
            P(("sub", "grp"), None),
            P(("sub", "grp"), None, None),
            P(("sub", "grp"), None, None),
            P("sub", None),
        ),
        out_specs=(
            P(("sub", "grp"), None, None, None),
            P(("sub", "grp"), None, None, None),
            P(("sub", "grp"), None),
        ),
        check_vma=False,
    )
```

```python
import functools

import jax
import jax.numpy as jnp
from jax import lax
from jax.experimental import pallas as pl
from jax.experimental.pallas import tpu as pltpu
from jax.sharding import PartitionSpec as P

NY = 8
NZ = 8
CV_DEV = 4
ITERS = 3
RELAXATION = 0.5
DEPTH = 640
AXES = ("sub", "grp")
F32 = jnp.float32
BF16 = jnp.bfloat16
VMEM = pl.BlockSpec(memory_space=pltpu.VMEM)
HBM = pl.BlockSpec(memory_space=pltpu.HBM)
SMEM = pl.BlockSpec(memory_space=pltpu.SMEM)
PARAMS = pltpu.CompilerParams(vmem_limit_bytes=24 * 1024 * 1024)
STAGE = pltpu.CompilerParams(vmem_limit_bytes=50 * 1024 * 1024)
WHOLE = pltpu.CompilerParams(vmem_limit_bytes=56 * 1024 * 1024)


def position():
    place = lax.axis_index(AXES)
    odd = lax.rem(place, 2)
    has_left = (place > 0).astype(F32)
    has_right = (place < lax.axis_size(AXES) - 1).astype(F32)
    return odd, has_left, has_right


def swap_pairs(count):
    near = [(i, i ^ 1) for i in range(count)]
    far = []
    for i in range(1, count - 1, 2):
        far += [(i, i + 1), (i + 1, i)]
    return near, far


def pack_kernel(shear_hbm, ratio_hbm, labels_hbm, basis_hbm, coarse_hbm,
                far_ref, near_ref, mats_ref, rows_ref, wide_ref,
                shear_ref, ratio_ref, labels_ref, basis_ref, coarse_ref, sems):
    planes, nodes = labels_ref.shape
    plane_rows = 3 * NY * NZ
    moves = [
        (labels_hbm, labels_ref),
        (shear_hbm, shear_ref),
        (ratio_hbm, ratio_ref),
        (basis_hbm, basis_ref),
        (coarse_hbm, coarse_ref),
    ]
    copies = [pltpu.make_async_copy(source, target, sems.at[i]) for i, (source, target) in enumerate(moves)]
    for copy in copies:
        copy.start()
    odd = position()[0] == 1
    wide_ref[...] = jnp.zeros_like(wide_ref)
    for copy in copies:
        copy.wait()
    labels = labels_ref[...]
    shear = jnp.zeros((planes, nodes), F32)
    normal = jnp.zeros((planes, nodes), F32)
    for region in range(shear_ref.shape[1]):
        value = shear_ref[:, region : region + 1]
        here = labels == region
        shear = jnp.where(here, value, shear)
        normal = jnp.where(here, value * (2.0 + ratio_ref[:, region : region + 1]), normal)
    both = jnp.concatenate([shear, normal], axis=1)
    mats_ref[...] = both
    mats_l, mats_r = both[:2], both[planes - 2 :]
    groups = group_count(plane_rows, coarse_ref.shape[1])
    far_ref[8 * groups : 8 * groups + 2] = jnp.where(odd, mats_r, mats_l)
    near_ref[8 * groups : 8 * groups + 2] = jnp.where(odd, mats_l, mats_r)
    far_ref[8 * groups + 2 :] = jnp.zeros_like(far_ref[8 * groups + 2 :])
    near_ref[8 * groups + 2 :] = jnp.zeros_like(near_ref[8 * groups + 2 :])
    wide_ref[:, plane_rows : plane_rows + basis_ref.shape[1]] = basis_ref[...]
    rows = coarse_ref[:CV_DEV]
    for member in range(1, coarse_ref.shape[0] // CV_DEV):
        rows = jnp.where(lax.axis_index("grp") == member, coarse_ref[member * CV_DEV : (member + 1) * CV_DEV], rows)
    rows_ref[...] = rows
    span = part_blocks(plane_rows)
    start_r = planes * plane_rows
    start_l = 4 * plane_rows - 128 * span
    nothing = jnp.zeros((CV_DEV, 128), F32)
    for i in range(groups):
        at = 8 * i
        block_l = block_r = row = nothing
        if i < span:
            block_l = wide_ref[:, start_l + 128 * i : start_l + 128 * (i + 1)]
            block_r = wide_ref[:, start_r + 128 * i : start_r + 128 * (i + 1)]
        if i * 128 < coarse_ref.shape[1]:
            row = rows[:, 128 * i : 128 * (i + 1)]
        far_ref[at : at + CV_DEV] = jnp.where(odd, block_r, block_l)
        near_ref[at : at + CV_DEV] = jnp.where(odd, block_l, block_r)
        far_ref[at + CV_DEV : at + 2 * CV_DEV] = row
        near_ref[at + CV_DEV : at + 2 * CV_DEV] = row


def stage_kernel(inverse_hbm, inverse_ref, sems):
    step = inverse_ref.shape[0] // 3
    copies = []
    for i in range(3):
        part = pl.ds(i * step, step)
        copies.append(pltpu.make_async_copy(inverse_hbm.at[part, :], inverse_ref.at[part, :], sems.at[i]))
    for copy in copies:
        copy.start()
    for copy in copies:
        copy.wait()


def on_lanes(row, shape):
    return jnp.transpose(jnp.broadcast_to(row, (shape[-1], row.shape[1]))).reshape(shape[1:])


def part_blocks(plane_rows):
    return -(-3 * plane_rows // 128)


def group_count(plane_rows, coarse_order):
    return max(part_blocks(plane_rows), coarse_order // 128)


def up_a(u):
    return jnp.concatenate([u[1:], jnp.zeros_like(u[:1])], axis=0)


def down_a(u):
    return jnp.concatenate([jnp.zeros_like(u[:1]), u[:-1]], axis=0)


def up_b(u):
    return pltpu.roll(u, NZ - 1, 1)


def down_b(u):
    return pltpu.roll(u, 1, 1)


def stencil_plane(mats, plane, field):
    b = lax.broadcasted_iota(jnp.int32, (NY, NZ, mats.shape[-1]), 1)
    last, first = b == NZ - 1, b == 0
    near_a, near_b_up, near_b_down, along, diagonal = [], [], [], [], []
    for kind in range(2):
        s = mats[plane, kind]
        half = 0.5 * s
        k_up = 0.5 * up_a(s) + half
        k_down = 0.5 * down_a(s) + half
        b_up = jnp.where(last, 0.0, 0.5 * up_b(s) + half)
        b_down = jnp.where(first, 0.0, 0.5 * down_b(s) + half)
        p_up = 0.5 * mats[plane + 1, kind] + half
        p_down = 0.5 * mats[plane - 1, kind] + half
        near_a.append((k_up, k_down))
        near_b_up.append(b_up)
        near_b_down.append(b_down)
        along.append((p_up, p_down))
        edge = jnp.where(last | first, half, 0.0)
        diagonal.append((p_up + p_down, k_up + k_down, b_up + b_down + edge))
    results = []
    for component in range(3):
        kinds = [1 if dimension == component else 0 for dimension in range(3)]
        u = field(plane, component)
        total = (diagonal[kinds[0]][0] + diagonal[kinds[1]][1] + diagonal[kinds[2]][2]) * u
        total = total - along[kinds[0]][0] * field(plane + 1, component)
        total = total - along[kinds[0]][1] * field(plane - 1, component)
        total = total - near_a[kinds[1]][0] * up_a(u)
        total = total - near_a[kinds[1]][1] * down_a(u)
        total = total - near_b_up[kinds[2]] * up_b(u)
        total = total - near_b_down[kinds[2]] * down_b(u)
        results.append(total)
    return results


def split(x):
    high = x.astype(BF16)
    return high, (x - high.astype(F32)).astype(BF16)


def block(plane, component):
    start = (plane * 3 + component) * NY * NZ
    return slice(start, start + NY * NZ)


def node_grid(rows):
    return rows.reshape(rows.shape[0] // (NY * NZ), NY, NZ, rows.shape[1])


def products(width, order_ref, inverse_ref, basis_ref, ordered_ref, product_ref, res_ref, t_ref, far_ref, near_ref,
             q_ref):
    size = res_ref.shape[0]
    step = size // 3
    for start in range(0, size, DEPTH):
        chunk = slice(start, min(start + DEPTH, size))
        for row in range(chunk.start, chunk.stop):
            ordered_ref[row : row + 1, :] = res_ref[pl.ds(order_ref[0, row], 1), :]
        ordered = ordered_ref[chunk, :].astype(BF16)
        for i in range(3):
            part = slice(i * step, (i + 1) * step)
            value = jnp.dot(inverse_ref[part, chunk], ordered, preferred_element_type=F32)
            product_ref[part, :] = value if start == 0 else product_ref[part, :] + value
            if chunk.stop == size:
                for row in range(part.start, part.stop):
                    t_ref[pl.ds(order_ref[0, row], 1), :] = product_ref[row : row + 1, :]
    odd, _, _ = position()
    to_right = size - width
    far_ref[:width] = t_ref[pl.ds(pl.multiple_of(to_right * odd, 8), width), :]
    near_ref[:width] = t_ref[pl.ds(pl.multiple_of(to_right * (1 - odd), 8), width), :]
    high, low = split(res_ref[...])
    b_high, b_low = split(basis_ref[...])
    both = jnp.concatenate([b_high, b_low], axis=0)
    first = jnp.dot(both, high, preferred_element_type=F32)
    second = jnp.dot(both, low, preferred_element_type=F32)
    half = basis_ref.shape[0]
    q = (first[:half] + second[:half] + first[half:])[:CV_DEV]
    q_ref[...] = jnp.broadcast_to(q[None], q_ref.shape)


def first_kernel(order_ref, loads_ref, far_in_ref, near_in_ref, far_pack_ref, near_pack_ref, inverse_ref, basis_ref,
                 res_ref, t_ref, far_ref, near_ref, q_ref, ordered_ref, product_ref):
    plane_rows = 3 * NY * NZ
    planes = loads_ref.shape[0] // plane_rows
    odd = position()[0] == 1
    far, near = far_in_ref[...], near_in_ref[...]
    res_ref[:plane_rows] = jnp.where(odd, near, far)
    res_ref[plane_rows : (planes + 1) * plane_rows] = loads_ref[...]
    res_ref[(planes + 1) * plane_rows :] = jnp.where(odd, far, near)
    far_ref[3 * plane_rows :] = far_pack_ref[...]
    near_ref[3 * plane_rows :] = near_pack_ref[...]
    products(3 * plane_rows, order_ref, inverse_ref, basis_ref, ordered_ref, product_ref, res_ref, t_ref, far_ref,
             near_ref, q_ref)


def unpack(far_in_ref, near_in_ref, mats_in_ref, wide_ref, own_rows_ref, mats_ref, extent_ref, rows_ref):
    plane_rows = 3 * NY * NZ
    odd = position()[0] == 1

    def beside(start, stop):
        start, stop = 3 * plane_rows + start, 3 * plane_rows + stop
        far, near = far_in_ref[start:stop], near_in_ref[start:stop]
        return jnp.where(odd, near, far), jnp.where(odd, far, near)

    extent = extent_ref.shape[1]
    span = part_blocks(plane_rows)
    extent_ref[...] = jnp.zeros_like(extent_ref)
    rows_ref[...] = jnp.zeros_like(rows_ref)
    extent_ref[CV_DEV : 2 * CV_DEV] = wide_ref[...]
    rows_ref[CV_DEV : 2 * CV_DEV] = own_rows_ref[...]
    groups = group_count(plane_rows, rows_ref.shape[1])
    for i in range(groups):
        at = 8 * i
        if i < span:
            left, right = beside(at, at + CV_DEV)
            extent_ref[:CV_DEV, 128 * i : 128 * (i + 1)] = left
            start = extent - 128 * span + 128 * i
            extent_ref[2 * CV_DEV : 3 * CV_DEV, start : start + 128] = right
        if i * 128 < rows_ref.shape[1]:
            left, right = beside(at + CV_DEV, at + 2 * CV_DEV)
            rows_ref[:CV_DEV, 128 * i : 128 * (i + 1)] = left
            rows_ref[2 * CV_DEV : 3 * CV_DEV, 128 * i : 128 * (i + 1)] = right
    left, right = beside(8 * groups, 8 * groups + 2)
    planes = mats_in_ref.shape[0]
    for plane in range(2):
        mats_ref[plane] = on_lanes(left[plane : plane + 1], mats_ref.shape)
        mats_ref[planes + 2 + plane] = on_lanes(right[plane : plane + 1], mats_ref.shape)
    for plane in range(planes):
        mats_ref[2 + plane] = on_lanes(mats_in_ref[plane : plane + 1], mats_ref.shape)


def correction(width, q_ref, rows_ref, extent_ref, t_ref, far_ref, near_ref, z_ref):
    plane_rows = 3 * NY * NZ
    out_planes = t_ref.shape[0] // plane_rows + 2
    coarse = jnp.dot(rows_ref[...], q_ref[...], precision=lax.Precision.HIGHEST, preferred_element_type=F32)
    c_high, c_low = split(coarse)
    e_high, e_low = split(extent_ref[...])
    spread = lax.dot_general(
        jnp.concatenate([e_high, e_low, e_high], axis=0),
        jnp.concatenate([c_high, c_high, c_low], axis=0),
        (((0,), (0,)), ((), ())),
        preferred_element_type=F32,
    )
    odd, has_left, has_right = position()
    odd = odd == 1

    def rows_at(ref, plane):
        return ref[plane * plane_rows : (plane + 1) * plane_rows]

    for plane in range(3 - width, out_planes - 3 + width):
        value = spread[plane * plane_rows : (plane + 1) * plane_rows]
        if 1 <= plane < out_planes - 1:
            value = value + rows_at(t_ref, plane - 1)
        if plane < 3:
            at = plane - (3 - width)
            value = value + jnp.where(odd, rows_at(near_ref, at), rows_at(far_ref, at))
        if plane >= out_planes - 3:
            at = plane - (out_planes - 3)
            value = value + jnp.where(odd, rows_at(far_ref, at), rows_at(near_ref, at))
        if plane < 2:
            value = value * has_left
        if plane >= out_planes - 2:
            value = value * has_right
        z_ref[plane] = node_grid(value)
    return coarse


def second_kernel(width, order_ref, q_in_ref, mats_in_ref, wide_ref, own_rows_ref, t_in_ref, far_in_ref, near_in_ref,
                  res_in_ref, inverse_ref, basis_ref, solution_ref, res_ref, t_ref, far_ref, near_ref, q_ref,
                  mats_ref, extent_ref, rows_ref, *scratch):
    unpack(far_in_ref, near_in_ref, mats_in_ref, wide_ref, own_rows_ref, mats_ref, extent_ref, rows_ref)
    middle_kernel(width, order_ref, q_in_ref, rows_ref, extent_ref, mats_ref, t_in_ref, far_in_ref, near_in_ref,
                  res_in_ref, None, inverse_ref, basis_ref, solution_ref, res_ref, t_ref, far_ref, near_ref, q_ref,
                  *scratch)


def middle_kernel(width, order_ref, q_in_ref, rows_ref, extent_ref, mats_ref, t_in_ref, far_in_ref, near_in_ref,
                  res_in_ref, solution_in_ref, inverse_ref, basis_ref, solution_ref, res_ref, t_ref, far_ref,
                  near_ref, q_ref, z_ref, *scratch):
    correction(3, q_in_ref, rows_ref, extent_ref, t_in_ref, far_in_ref, near_in_ref, z_ref)
    _, has_left, has_right = position()
    window = z_ref.shape[0] - 2
    for plane in range(1, window + 1):
        applied = stencil_plane(mats_ref, plane, lambda p, c: z_ref[p, c])
        for component in range(3):
            at = block(plane - 1, component)
            value = res_in_ref[at] - RELAXATION * applied[component].reshape(NY * NZ, res_ref.shape[1])
            if plane == 1:
                value = value * has_left
            if plane == window:
                value = value * has_right
            res_ref[at] = value
    own = RELAXATION * z_ref[2:window].reshape(solution_ref.shape)
    solution_ref[...] = own if solution_in_ref is None else solution_in_ref[...] + own
    products(width * 3 * NY * NZ, order_ref, inverse_ref, basis_ref, *scratch, res_ref, t_ref, far_ref, near_ref, q_ref)


def last_kernel(q_in_ref, rows_ref, extent_ref, mats_ref, t_in_ref, far_in_ref, near_in_ref, res_in_ref,
                solution_in_ref, solution_ref, residual_ref, coarse_ref, z_ref):
    coarse = correction(2, q_in_ref, rows_ref, extent_ref, t_in_ref, far_in_ref, near_in_ref, z_ref)
    coarse_ref[...] = coarse[CV_DEV : 2 * CV_DEV]
    planes = z_ref.shape[0] - 4
    solution_ref[...] = solution_in_ref[...] + RELAXATION * z_ref[2 : planes + 2].reshape(solution_ref.shape)
    for plane in range(2, planes + 2):
        applied = stencil_plane(mats_ref, plane, lambda p, c: z_ref[p, c])
        for component in range(3):
            residual_ref[block(plane - 2, component)] = res_in_ref[
                block(plane - 1, component)
            ] - RELAXATION * applied[component].reshape(NY * NZ, residual_ref.shape[1])


def body(
    applied_loads,
    labels,
    shear_modulus,
    stiff_ratio,
    local_order,
    local_inverse,
    coarse_basis,
    coarse_inverse,
):
    planes, components, nodes, cases = applied_loads.shape
    window = planes + 2
    plane_rows = components * nodes
    size = window * plane_rows
    coarse_order = coarse_inverse.shape[1]
    count = lax.axis_size(AXES)
    near_pairs, far_pairs = swap_pairs(count)
    basis = coarse_basis[0]
    basis_pad = jnp.pad(basis, ((0, 16 - CV_DEV), (0, 0)))
    extent = size + 2 * plane_rows

    odd = lax.rem(lax.axis_index(AXES), 2)

    def loads_plane(plane):
        return lax.dynamic_index_in_dim(applied_loads, plane, 0, keepdims=False).reshape(plane_rows, cases)

    far_in = lax.ppermute(loads_plane((planes - 1) * odd), AXES, far_pairs)
    near_in = lax.ppermute(loads_plane((planes - 1) * (1 - odd)), AXES, near_pairs)

    pack_rows = 8 * group_count(plane_rows, coarse_order) + 8
    packed = jax.ShapeDtypeStruct((pack_rows, cases), F32)
    far_pack, near_pack, mats_own, own_rows, wide = pl.pallas_call(
        pack_kernel,
        out_shape=[
            packed,
            packed,
            jax.ShapeDtypeStruct((planes, 2 * nodes), F32),
            jax.ShapeDtypeStruct((CV_DEV, coarse_order), F32),
            jax.ShapeDtypeStruct((CV_DEV, extent), F32),
        ],
        in_specs=[HBM] * 5,
        out_specs=[VMEM] * 5,
        scratch_shapes=[
            pltpu.VMEM((1, shear_modulus.shape[0]), F32),
            pltpu.VMEM((1, shear_modulus.shape[0]), F32),
            pltpu.VMEM((planes, nodes), jnp.int32),
            pltpu.VMEM((CV_DEV, size), F32),
            pltpu.VMEM(coarse_inverse.shape, F32),
            pltpu.SemaphoreType.DMA((5,)),
        ],
        compiler_params=WHOLE,
        cost_estimate=pl.CostEstimate(flops=8 * size**3, bytes_accessed=4 * size * size, transcendentals=0),
    )(shear_modulus[None], stiff_ratio[None], labels, basis, coarse_inverse)

    def field(depth):
        return jax.ShapeDtypeStruct((depth * plane_rows, cases), F32)

    q_shape = jax.ShapeDtypeStruct((count, CV_DEV, cases), F32)
    cost = pl.CostEstimate(flops=2 * size * size * cases, bytes_accessed=2 * size * size, transcendentals=0)
    z_scratch = pltpu.VMEM((planes + 4, components, NY, NZ, cases), F32)
    scratch = [pltpu.VMEM((size, cases), F32), pltpu.VMEM((size, cases), F32)]
    loads = applied_loads.reshape(planes * plane_rows, cases)

    def move(far_out, near_out, q):
        far_in = lax.ppermute(far_out, AXES, far_pairs)
        near_in = lax.ppermute(near_out, AXES, near_pairs)
        q_all = lax.all_to_all(q, AXES, 0, 0).reshape(count * CV_DEV, cases)
        return far_in, near_in, q_all

    inverse = pl.pallas_call(
        stage_kernel,
        out_shape=jax.ShapeDtypeStruct((size, size), BF16),
        in_specs=[HBM],
        out_specs=VMEM,
        scratch_shapes=[pltpu.SemaphoreType.DMA((3,))],
        compiler_params=STAGE,
        cost_estimate=pl.CostEstimate(flops=4 * size**3, bytes_accessed=4 * size * size, transcendentals=0),
    )(local_inverse[0])
    carried = jax.ShapeDtypeStruct((3 * plane_rows + pack_rows, cases), F32)
    res, t, far_out, near_out, q = pl.pallas_call(
        first_kernel,
        out_shape=[field(window), field(window), carried, carried, q_shape],
        in_specs=[SMEM] + [VMEM] * 7,
        out_specs=[VMEM] * 5,
        scratch_shapes=scratch,
        compiler_params=PARAMS,
        cost_estimate=cost,
    )(local_order, loads, far_in, near_in, far_pack, near_pack, inverse, basis_pad)
    far_in, near_in, q_all = move(far_out, near_out, q)
    for iteration in range(1, ITERS):
        width = 2 if iteration == ITERS - 1 else 3
        outs = [field(planes), field(window), field(window), field(width), field(width), q_shape]
        if iteration == 1:
            kernel = second_kernel
            operands = [local_order, q_all, mats_own, wide, own_rows, t, far_in, near_in, res, inverse, basis_pad]
            outs += [
                jax.ShapeDtypeStruct((planes + 4, 2, NY, NZ, cases), F32),
                jax.ShapeDtypeStruct((16, extent), F32),
                jax.ShapeDtypeStruct((16, coarse_order), F32),
            ]
        else:
            kernel = middle_kernel
            operands = [local_order, q_all, inverse_rows, extents, mats_all, t, far_in, near_in, res, solution,
                        inverse, basis_pad]
        solution, res, t, far_out, near_out, q, *setup = pl.pallas_call(
            functools.partial(kernel, width),
            out_shape=outs,
            in_specs=[SMEM] + [VMEM] * (len(operands) - 1),
            out_specs=[VMEM] * len(outs),
            scratch_shapes=[z_scratch, *scratch],
            compiler_params=PARAMS,
            cost_estimate=cost,
        )(*operands)
        if setup:
            mats_all, extents, inverse_rows = setup
        far_in, near_in, q_all = move(far_out, near_out, q)
    solution, residual, coarse_values = pl.pallas_call(
        last_kernel,
        out_shape=[field(planes), field(planes), jax.ShapeDtypeStruct((CV_DEV, cases), F32)],
        in_specs=[VMEM] * 9,
        out_specs=[VMEM] * 3,
        scratch_shapes=[z_scratch],
        compiler_params=PARAMS,
    )(q_all, inverse_rows, extents, mats_all, t, far_in, near_in, res, solution)
    return (
        solution.reshape(planes, components, nodes, cases),
        residual.reshape(planes, components, nodes, cases),
        coarse_values,
    )


def solution(mesh):
    return jax.shard_map(
        body,
        mesh=mesh,
        in_specs=(
            P(("sub", "grp"), None, None, None),
            P(("sub", "grp"), None),
            P(),
            P(),
            P(("sub", "grp"), None),
            P(("sub", "grp"), None, None),
            P(("sub", "grp"), None, None),
            P("sub", None),
        ),
        out_specs=(
            P(("sub", "grp"), None, None, None),
            P(("sub", "grp"), None, None, None),
            P(("sub", "grp"), None),
        ),
        check_vma=False,
    )
```
